512 devices in a mesh: row: 16 (over y, x), col: 32 (over z, core).
Axes of the slice: x: 4, y: 4, z: 16, core: 2. Of those that a mesh axis runs over, the one named last changes fastest.
Arguments:
- tokens: bfloat16 [512, 12288], P('col', 'row'), may hold values from -6 to 6
- up_proj: bfloat16 [12288, 24576], P('row', 'col'), may hold values from -0.109375 to 0.109375
- down_proj: bfloat16 [24576, 12288], P('col', 'row'), may hold values from -0.078125 to 0.078125
- keep_mask: int32 [96, 192], P('row', 'col'), may hold values from 0 to 1, as said below
- cotangent: bfloat16 [512, 12288], P('col', 'row'), may hold values from -3 to 3
Outputs:
- output: bfloat16 [512, 12288], P('col', 'row')
- input_grad: bfloat16 [512, 12288], P('col', 'row')
- up_grad: bfloat16 [12288, 24576], P('row', 'col')
- down_grad: bfloat16 [24576, 12288], P('col', 'row')
The draws below stay inside these ranges and needn't reach their ends.
Inputs may be any that keep to these rules, and one draw needn't show every extreme that they name: `keep_mask`: the device grid cuts the mask into tiles of (12288 / 128 / 16) x (24576 / 128 / 32) blocks, split as up_proj; a tile keeps at most 24 blocks and some tile keeps exactly 24; tiles may keep none.
All inputs are finite; a program needn't handle non-finite values.
Results may differ from the reference program's by a relative error of at most 0.034.
Values may be sent and summed in bfloat16 or wider, within the bound.
A program may use at most 128 MiB of HBM per device.

```python
import jax
import jax.numpy as jnp
from jax import lax

D = 12288
FFW = 24576
BLOCK = 128
TOKENS = 512
N_ROW = 16
N_COL = 32


def draw_keep_mask(key, part):
    key = jax.random.fold_in(key, 7)
    tile_rows = D // BLOCK // N_ROW
    tile_cols = FFW // BLOCK // N_COL
    tile_count = N_ROW * N_COL
    per_tile = tile_rows * tile_cols
    quarter = per_tile // 4
    largest = per_tile * 2 // 3
    first_key, second_key, third_key = jax.random.split(key, 3)
    counts = jax.random.randint(first_key, (tile_count,), 0, 2 * quarter + 1)
    fullest = jax.random.randint(second_key, (), 0, tile_count)
    counts = jnp.where(jnp.arange(tile_count) == fullest, largest, counts)
    ranking = jax.vmap(lambda sub_key: jax.random.permutation(sub_key, per_tile))(jax.random.split(third_key, tile_count))
    kept_blocks = (ranking < counts[:, None]).astype(jnp.int32)
    kept_blocks = kept_blocks.reshape(N_ROW, N_COL, tile_rows, tile_cols).transpose(0, 2, 1, 3)
    return kept_blocks.reshape(N_ROW * tile_rows, N_COL * tile_cols)


def block_levels(rng, shape, pieces, low, top_value):
    def one(position, blocks):
        steps = jax.random.uniform(jax.random.fold_in(jax.random.fold_in(rng, 6), position), (blocks,), jnp.float32, low / len(pieces), top_value / len(pieces))
        return jnp.repeat(jnp.exp(steps), shape[position] // blocks).reshape((-1,) + (1,) * (len(shape) - position - 1))

    gain = one(*pieces[0])
    for cut in pieces[1:]:
        gain = gain * one(*cut)
    return gain


def bell_draw(own_key, dims, scale, limit, shards=(), kind=jnp.bfloat16):
    result = jax.random.normal(own_key, dims, jnp.float32) * scale
    if len(shards) > 0:
        result = block_levels(own_key, dims, shards, -0.22, 0.18) * result
    return jnp.clip(result, min=-limit, max=limit).astype(kind)


def setup_inputs(seed: int = 0) -> dict:
    arg_keys = jax.random.split(jax.random.key(seed), 6)
    return {
        "tokens": bell_draw(arg_keys[0], (TOKENS, D), 1.0, 6.0, ((0, 32), (1, 16))),
        "up_proj": bell_draw(arg_keys[1], (D, FFW), (D // 4) ** -0.5, 0.109375, ((0, 16), (1, 32))),
        "down_proj": bell_draw(arg_keys[2], (FFW, D), (FFW // 4) ** -0.5, 0.078125, ((0, 32), (1, 16))),
        "keep_mask": draw_keep_mask(jax.random.fold_in(arg_keys[5], 71), 0),
        "cotangent": bell_draw(arg_keys[4], (TOKENS, D), 0.5, 3.0, ((0, 32), (1, 16))),
    }


def expand_mask(keep_mask):
    grown = jnp.repeat(jnp.repeat(keep_mask, BLOCK, axis=0), BLOCK, axis=1)
    return grown.astype(jnp.bfloat16)

def gelu_pull(hidden, upstream):
    pullback = jax.vjp(lambda values: jax.nn.gelu(values, approximate=True), hidden)[1]
    return pullback(upstream)[0]

def grouped_product(left, right, groups):
    width = left.shape[1] // groups

    def add_group(total, index):
        left_part = lax.dynamic_slice_in_dim(left, index * width, width, 1)
        right_part = lax.dynamic_slice_in_dim(right, index * width, width, 0)
        term = jnp.dot(left_part, right_part, precision=lax.Precision.HIGHEST)
        rounded = lax.optimization_barrier(term.astype(jnp.bfloat16))
        return (total + rounded.astype(jnp.float32), None)
    start = jnp.zeros((left.shape[0], right.shape[1]), jnp.float32)
    total, _ = lax.scan(add_group, start, jnp.arange(groups, dtype=jnp.int32))
    return total

def reference(tokens, up_proj, down_proj, keep_mask, cotangent):
    masked = expand_mask(keep_mask)
    up_masked = (up_proj * masked).astype(jnp.float32)
    down_masked = (down_proj * masked.T).astype(jnp.float32)
    tok_float = tokens.astype(jnp.float32)
    cot_float = cotangent.astype(jnp.float32)
    best = lax.Precision.HIGHEST
    hidden = grouped_product(tok_float, up_masked, N_ROW)
    active = jax.nn.gelu(hidden, approximate=True).astype(jnp.bfloat16)
    act_float = active.astype(jnp.float32)
    output = grouped_product(act_float, down_masked, N_COL).astype(jnp.bfloat16)
    upstream = grouped_product(cot_float, down_masked.T, N_ROW)
    hidden_grad = gelu_pull(hidden, upstream).astype(jnp.bfloat16)
    grad_float = hidden_grad.astype(jnp.float32)
    mask_float = masked.astype(jnp.float32)
    down_grad = (jnp.dot(act_float.T, cot_float, precision=best) * mask_float.T).astype(jnp.bfloat16)
    up_grad = (jnp.dot(tok_float.T, grad_float, precision=best) * mask_float).astype(jnp.bfloat16)
    input_grad = grouped_product(grad_float, up_masked.T, N_COL).astype(jnp.bfloat16)
    return (output, input_grad, up_grad, down_grad)
```

```python
import jax
import jax.numpy as jnp
from jax import lax
from jax.experimental import pallas as pl
from jax.experimental.pallas import tpu as pltpu
from jax.sharding import PartitionSpec as P

MESH = pl.DeviceIdType.MESH
F32 = jnp.float32
BF16 = jnp.bfloat16
B = 128
T = 16
W = 768
NB = W // B
HALF = W // 2
CH = 256
N_CH = W // CH

AG_PER = 18
S1, S2, G1, G2 = 0, 12, 24, 36
R1, R2 = 48, 56
D_UP, D_DN, D_TOK, D_COT, D_ACT, D_HG = 62, 63, 64, 65, 66, 67
N_SEM = 68

GELU_C = 0.7978845608028654
GELU_A = 0.044715


def kernel(tok_ref, up_hbm, down_hbm, mask_ref, cot_ref, out_ref, in_ref, upg_hbm, dng_hbm,
           wup, wdn, ag, part, s1buf, s2buf, acts, pacts, zpart, r1buf, r1sum, r2buf, gbuf,
           ag_send, ag_recv, send, recv, loc):
    row = lax.axis_index("row")
    col = lax.axis_index("col")
    x, y = row % 4, row // 4
    z, k = col // 2, col % 2
    other = 1 - k

    def zdev(d):
        return (row, ((z + d + 16) % 16) * 2 + k)

    def xdev(d):
        return (y * 4 + (x + d) % 4, col)

    def ydev(d):
        return (((y + d) % 4) * 4 + x, col)

    mate = (row, z * 2 + other)

    cp_up = pltpu.make_async_copy(up_hbm, wup.at[k], loc.at[0])
    cp_dn = pltpu.make_async_copy(down_hbm, wdn.at[k], loc.at[1])
    cp_up.start()
    cp_dn.start()

    peers = [zdev(d) for d in (4, -4, 1, -1, 2, -2)] + [xdev(d) for d in (1, 2, 3)] + [ydev(d) for d in (1, 2, 3)] + [mate]
    barrier = pltpu.get_barrier_semaphore()
    for peer in peers:
        pl.semaphore_signal(barrier, inc=1, device_id=peer, device_id_type=MESH)

    def pair_rows(zb):
        zz = (zb + 32) % 16
        return pl.multiple_of((zz % 4) * 64 + ((zz // 4) % 2) * 32, 32)

    def class_rows(zb):
        return pl.multiple_of(((zb + 32) % 4) * 64, 64)

    def block_pos(zb):
        zz = (zb + 32) % 16
        return (zz % 4) * 4 + ((zz // 4) % 2) * 2 + zz // 8

    def block_rows(zb):
        return pl.multiple_of(block_pos(zb) * T, T)

    ag[0, k, pl.ds(block_rows(z), T), :] = tok_ref[...]
    ag[1, k, pl.ds(block_rows(z), T), :] = cot_ref[...]
    cp_up.wait()
    for i in range(NB):
        for j in range(NB):
            m = mask_ref[i, j].astype(F32).astype(BF16)
            wup[k, B * i:B * (i + 1), B * j:B * (j + 1)] = wup[k, B * i:B * (i + 1), B * j:B * (j + 1)] * m
    cp_dn.wait()
    for i in range(NB):
        for j in range(NB):
            m = mask_ref[i, j].astype(F32).astype(BF16)
            wdn[k, B * j:B * (j + 1), B * i:B * (i + 1)] = wdn[k, B * j:B * (j + 1), B * i:B * (i + 1)] * m

    pl.semaphore_wait(barrier, len(peers))

    sends = []

    def push(src, dst, s, r, device):
        copy = pltpu.make_async_remote_copy(src_ref=src, dst_ref=dst, send_sem=s, recv_sem=r, device_id=device, device_id_type=MESH)
        copy.start()
        sends.append(copy)

    def got(dst, s, r):
        pltpu.make_async_remote_copy(src_ref=dst, dst_ref=dst, send_sem=s, recv_sem=r, device_id=mate, device_id_type=MESH).wait_recv()

    def ag_block(a, zb):
        return ag.at[a, k, pl.ds(block_rows(zb), T), :]

    counts = [0, 0]

    def ag_push(a, zb, d):
        n = counts[a]
        counts[a] = n + 1
        push(ag_block(a, zb), ag_block(a, zb), ag_send.at[a * AG_PER + n], ag_recv.at[a * AG_PER + block_pos(zb)], zdev(d))

    def ag_got(a, zb):
        got(ag_block(a, zb), ag_send.at[0], ag_recv.at[a * AG_PER + block_pos(zb)])

    def half_block(a, zb, h):
        return ag.at[a, k, pl.ds(block_rows(zb), T), h * HALF:(h + 1) * HALF]

    for a in range(2):
        for d in (4, -4, 1, -1):
            ag_push(a, z, d)

    push(wup.at[k], wup.at[k], send.at[D_UP], recv.at[D_UP], mate)
    push(wdn.at[k], wdn.at[k], send.at[D_DN], recv.at[D_DN], mate)

    for a in range(2):
        for h, d in ((0, 4), (1, -4)):
            ag_got(a, z - d)
            n = counts[a]
            counts[a] = n + 1
            push(half_block(a, z - d, h), half_block(a, z - d, h), ag_send.at[a * AG_PER + n], ag_recv.at[a * AG_PER + 16 + h], zdev(d))
            for f in (2, -2, 1, -1):
                ag_push(a, z - d, f)
    for a in range(2):
        for h in range(2):
            got(half_block(a, z + 8, h), ag_send.at[0], ag_recv.at[a * AG_PER + 16 + h])
        for f in (1, -1):
            ag_push(a, z + 8, f)

    def ag_rest(a):
        for base in (2, 1, -1):
            for d in (0, 4, -4, 8):
                ag_got(a, z + base + d)
        push(ag.at[a, k], ag.at[a, k], send.at[(D_TOK, D_COT)[a]], recv.at[(D_TOK, D_COT)[a]], mate)

    axes = ((x, xdev, y, ydev), (y, ydev, x, xdev))

    def sem(base, a, h, d):
        i = base + (a * 2 + h) * 3 + d - 1
        return send.at[i], recv.at[i]

    def first_rows(h, d):
        return pl.ds(pl.multiple_of(((axes[h][0] + d) % 4) * 64, 64), 64)

    def second_rows(h, d):
        return pl.ds(pl.multiple_of(axes[h][0] * 64 + ((axes[h][2] + d) % 4) * T, T), T)

    def partial_and_send(a):
        for h in range(2):
            for n in range(N_CH):
                c = slice(n * CH, (n + 1) * CH)
                if a == 0:
                    v = jnp.dot(ag[0, k], wup[h, :, c], preferred_element_type=F32)
                else:
                    v = lax.dot_general(ag[1, k], wdn[h, c, :], (((1,), (1,)), ((), ())), preferred_element_type=F32)
                part[a, h, :, c] = v.astype(BF16)
            for d in (2, 1, 3):
                s, r = sem(S1, a, h, d)
                push(part.at[a, h, first_rows(h, d), :], s1buf.at[a, h, d - 1], s, r, axes[h][1](d))

    def second_stage(a):
        for h in range(2):
            for d in (1, 2, 3):
                got(s1buf.at[a, h, d - 1], *sem(S1, a, h, d))
            total = part[a, h, first_rows(h, 0), :].astype(F32)
            for d in range(3):
                total = total + s1buf[a, h, d].astype(F32)
            part[a, h, first_rows(h, 0), :] = total.astype(BF16)
            for d in (2, 1, 3):
                s, r = sem(S2, a, h, d)
                push(part.at[a, h, second_rows(h, d), :], s2buf.at[a, h, d - 1], s, r, axes[h][3](d))

    def shard(a, h):
        for d in (1, 2, 3):
            got(s2buf.at[a, h, d - 1], *sem(S2, a, h, d))
        total = part[a, h, second_rows(h, 0), :].astype(F32)
        for d in range(3):
            total = total + s2buf[a, h, d].astype(F32)
        return total

    def spread(a, h, value):
        acts[a, h, second_rows(h, 0), :] = value.astype(BF16)
        for d in (2, 1, 3):
            s, r = sem(G1, a, h, d)
            push(acts.at[a, h, second_rows(h, 0), :], acts.at[a, h, second_rows(h, 0), :], s, r, axes[h][3](d))

    def spread_more(a):
        for h in range(2):
            for d in (1, 2, 3):
                got(acts.at[a, h, second_rows(h, -d + 4), :], *sem(G1, a, h, d))
            for d in (2, 1, 3):
                s, r = sem(G2, a, h, d)
                push(acts.at[a, h, first_rows(h, 0), :], acts.at[a, h, first_rows(h, 0), :], s, r, axes[h][1](d))

    def spread_end(a):
        for h in range(2):
            for d in (1, 2, 3):
                got(acts.at[a, h, first_rows(h, -d + 4), :], *sem(G2, a, h, d))

    def z_partial(a):
        for n in range(N_CH):
            c = slice(n * CH, (n + 1) * CH)
            if a == 0:
                v = jnp.dot(acts[0, 0], wdn[0, :, c], preferred_element_type=F32)
                v = v + jnp.dot(acts[0, 1], wdn[1, :, c], preferred_element_type=F32)
            else:
                dims = (((1,), (1,)), ((), ()))
                v = lax.dot_general(acts[1, 0], wup[0, c, :], dims, preferred_element_type=F32)
                v = v + lax.dot_general(acts[1, 1], wup[1, c, :], dims, preferred_element_type=F32)
            zpart[a, :, c] = v.astype(BF16)
        r = R1 + 4 * a
        push(zpart.at[a, pl.ds(pair_rows(z - 2), 32), :], r1buf.at[a, pl.ds(128, 32), :], send.at[r + 2], recv.at[r + 2], zdev(2))
        push(zpart.at[a, pl.ds(pair_rows(z + 2), 32), :], r1buf.at[a, pl.ds(160, 32), :], send.at[r + 3], recv.at[r + 3], zdev(-2))
        push(zpart.at[a, pl.ds(class_rows(z + 1), 64), :], r1buf.at[a, pl.ds(0, 64), :], send.at[r], recv.at[r], zdev(1))
        push(zpart.at[a, pl.ds(class_rows(z - 1), 64), :], r1buf.at[a, pl.ds(64, 64), :], send.at[r + 1], recv.at[r + 1], zdev(-1))
        d = (D_ACT, D_HG)[a]
        push(acts.at[a, other], pacts.at[a], send.at[d], recv.at[d], mate)

    def z_second(a):
        r = R1 + 4 * a
        got(r1buf.at[a, pl.ds(128, 32), :], send.at[r + 2], recv.at[r + 2])
        got(r1buf.at[a, pl.ds(160, 32), :], send.at[r + 3], recv.at[r + 3])
        got(r1buf.at[a, pl.ds(0, 64), :], send.at[r], recv.at[r])
        got(r1buf.at[a, pl.ds(64, 64), :], send.at[r + 1], recv.at[r + 1])
        cls = pl.ds(class_rows(z), 64)
        r1sum[a] = zpart[a, cls, :].astype(F32) + r1buf[a, 0:64, :].astype(F32) + r1buf[a, 64:128, :].astype(F32)
        far = pl.ds(pl.multiple_of(pair_rows(z + 4) - class_rows(z), 32), 32)
        r1sum[a, far, :] = r1sum[a, far, :] + r1buf[a, 128:160, :].astype(F32) + r1buf[a, 160:192, :].astype(F32)
        zpart[a, cls, :] = r1sum[a].astype(BF16)
        q = R2 + 3 * a
        for n, d in enumerate((8, 4, -4)):
            push(zpart.at[a, pl.ds(block_rows(z + d), T), :], r2buf.at[a, n], send.at[q + n], recv.at[q + n], zdev(d))

    def z_end(a, ref):
        q = R2 + 3 * a
        for n in range(3):
            got(r2buf.at[a, n], send.at[q + n], recv.at[q + n])
        mine = pl.ds(pl.multiple_of(block_rows(z) - class_rows(z), T), T)
        total = r1sum[a, mine, :]
        for n in range(3):
            total = total + r2buf[a, n].astype(F32)
        ref[...] = total.astype(BF16)

    def grads(a):
        i = (D_ACT, D_HG)[a]
        got(pacts.at[a], send.at[i], recv.at[i])
        dims = (((0,), (0,)), ((), ()))
        for n in range(N_CH):
            c = slice(n * CH, (n + 1) * CH)
            if a == 0:
                v = lax.dot_general(acts[0, k, :, c], ag[1, k], dims, preferred_element_type=F32)
                v = v + lax.dot_general(pacts[0, :, c], ag[1, other], dims, preferred_element_type=F32)
            else:
                v = lax.dot_general(ag[0, k, :, c], acts[1, k], dims, preferred_element_type=F32)
                v = v + lax.dot_general(ag[0, other, :, c], pacts[1], dims, preferred_element_type=F32)
            for i in range(CH // B):
                for j in range(NB):
                    p = n * (CH // B) + i
                    m = (mask_ref[j, p] if a == 0 else mask_ref[p, j]).astype(F32)
                    gbuf[a, B * p:B * (p + 1), B * j:B * (j + 1)] = (v[B * i:B * (i + 1), B * j:B * (j + 1)] * m).astype(BF16)

    ag_rest(0)
    got(wup.at[other], send.at[D_UP], recv.at[D_UP])
    partial_and_send(0)
    second_stage(0)
    ag_rest(1)
    got(wdn.at[other], send.at[D_DN], recv.at[D_DN])
    partial_and_send(1)
    pre = []
    for h in range(2):
        v = shard(0, h)
        t = jnp.tanh(GELU_C * (v + GELU_A * v * v * v))
        spread(0, h, 0.5 * v * (1.0 + t))
        pre.append(0.5 * (1.0 + t) + 0.5 * v * (1.0 - t * t) * (GELU_C * (1.0 + 3.0 * GELU_A * v * v)))
    spread_more(0)
    second_stage(1)
    for h in range(2):
        spread(1, h, pre[h] * shard(1, h))
    spread_end(0)
    z_partial(0)
    spread_more(1)
    got(ag.at[0, other], send.at[D_TOK], recv.at[D_TOK])
    got(ag.at[1, other], send.at[D_COT], recv.at[D_COT])
    z_second(0)
    spread_end(1)
    z_partial(1)
    grads(0)
    cp_dg = pltpu.make_async_copy(gbuf.at[0], dng_hbm, loc.at[0])
    cp_dg.start()
    z_second(1)
    grads(1)
    cp_ug = pltpu.make_async_copy(gbuf.at[1], upg_hbm, loc.at[1])
    cp_ug.start()
    z_end(0, out_ref)
    z_end(1, in_ref)
    cp_dg.wait()
    cp_ug.wait()
    for copy in sends:
        copy.wait_send()


def per_device(tokens, up_proj, down_proj, keep_mask, cotangent):
    vmem = pl.BlockSpec(memory_space=pltpu.VMEM)
    hbm = pl.BlockSpec(memory_space=pl.ANY)
    smem = pl.BlockSpec(memory_space=pltpu.SMEM)
    small = jax.ShapeDtypeStruct((T, W), BF16)
    big = jax.ShapeDtypeStruct((W, W), BF16)
    return pl.pallas_call(
        kernel,
        out_shape=(small, small, big, big),
        in_specs=[vmem, hbm, hbm, smem, vmem],
        out_specs=(vmem, vmem, hbm, hbm),
        scratch_shapes=[
            pltpu.VMEM((2, W, W), BF16),
            pltpu.VMEM((2, W, W), BF16),
            pltpu.VMEM((2, 2, 256, W), BF16),
            pltpu.VMEM((2, 2, 256, W), BF16),
            pltpu.VMEM((2, 2, 3, 64, W), BF16),
            pltpu.VMEM((2, 2, 3, T, W), BF16),
            pltpu.VMEM((2, 2, 256, W), BF16),
            pltpu.VMEM((2, 256, W), BF16),
            pltpu.VMEM((2, 256, W), BF16),
            pltpu.VMEM((2, 192, W), BF16),
            pltpu.VMEM((2, 64, W), F32),
            pltpu.VMEM((2, 3, T, W), BF16),
            pltpu.VMEM((2, W, W), BF16),
            pltpu.SemaphoreType.DMA((2 * AG_PER,)),
            pltpu.SemaphoreType.DMA((2 * AG_PER,)),
            pltpu.SemaphoreType.DMA((N_SEM,)),
            pltpu.SemaphoreType.DMA((N_SEM,)),
            pltpu.SemaphoreType.DMA((2,)),
        ],
        compiler_params=pltpu.CompilerParams(collective_id=0, has_side_effects=True, vmem_limit_bytes=40 * 2**20),
        cost_estimate=pl.CostEstimate(flops=3_700_000_000, bytes_accessed=5_000_000, transcendentals=30000),
        name="ffn",
    )(tokens, up_proj, down_proj, keep_mask, cotangent)


def solution(mesh):
    return jax.shard_map(
        per_device,
        mesh=mesh,
        in_specs=(P("col", "row"), P("row", "col"), P("col", "row"), P("row", "col"), P("col", "row")),
        out_specs=(P("col", "row"), P("col", "row"), P("row", "col"), P("col", "row")),
        check_vma=False,
    )
```

```python
import jax
import jax.numpy as jnp
from jax import lax
from jax.experimental import pallas as pl
from jax.experimental.pallas import tpu as pltpu
from jax.sharding import PartitionSpec as P

MESH = pl.DeviceIdType.MESH
F32 = jnp.float32
BF16 = jnp.bfloat16
B = 128
T = 16
W = 768
NB = W // B
HALF = W // 2
CH = 256
N_CH = W // CH

AG_PER = 18
S1, S2, G1, G2 = 0, 12, 24, 36
R1, R2 = 48, 56
D_UP, D_DN, D_TOK, D_COT, D_ACT, D_HG = 62, 63, 64, 65, 66, 67
N_SEM = 68

GELU_C = 0.7978845608028654
GELU_A = 0.044715


def kernel(tok_hbm, up_hbm, down_hbm, mask_hbm, cot_hbm, out_hbm, in_hbm, upg_hbm, dng_hbm,
           wup, wdn, ag, part, s1buf, s2buf, acts, pacts, zpart, r1buf, r1sum, r2buf, gbuf, obuf, mask_ref,
           ag_send, ag_recv, send, recv, loc, mate_sem):
    row = lax.axis_index("row")
    col = lax.axis_index("col")
    x, y = row % 4, row // 4
    z, k = col // 2, col % 2
    other = 1 - k

    def zdev(d):
        return (row, ((z + d + 16) % 16) * 2 + k)

    def xdev(d):
        return (y * 4 + (x + d) % 4, col)

    def ydev(d):
        return (((y + d) % 4) * 4 + x, col)

    mate = (row, z * 2 + other)

    def pair_rows(zb):
        zz = (zb + 32) % 16
        return pl.multiple_of((zz % 4) * 64 + ((zz // 4) % 2) * 32, 32)

    def class_rows(zb):
        return pl.multiple_of(((zb + 32) % 4) * 64, 64)

    def block_pos(zb):
        zz = (zb + 32) % 16
        return (zz % 4) * 4 + ((zz // 4) % 2) * 2 + zz // 8

    def block_rows(zb):
        return pl.multiple_of(block_pos(zb) * T, T)

    mine = pl.ds(block_rows(z), T)
    cp_tok = pltpu.make_async_copy(tok_hbm, ag.at[0, k, mine, :], loc.at[0])
    cp_cot = pltpu.make_async_copy(cot_hbm, ag.at[1, k, mine, :], loc.at[1])
    cp_mask = pltpu.make_async_copy(mask_hbm, mask_ref, loc.at[2])
    cp_up = pltpu.make_async_copy(up_hbm, wup.at[k], loc.at[3])
    cp_dn = pltpu.make_async_copy(down_hbm, wdn.at[k], loc.at[4])
    for cp in (cp_tok, cp_cot, cp_mask, cp_up, cp_dn):
        cp.start()

    peers = [zdev(d) for d in (4, -4, 1, -1, 2, -2)] + [xdev(d) for d in (1, 2, 3)] + [ydev(d) for d in (1, 2, 3)]
    barrier = pltpu.get_barrier_semaphore()
    for peer in peers:
        pl.semaphore_signal(barrier, inc=1, device_id=peer, device_id_type=MESH)

    @pl.when(k == 0)
    def _():
        pl.semaphore_signal(barrier, inc=1, device_id=mate, device_id_type=MESH)

    cp_tok.wait()
    cp_cot.wait()
    pl.semaphore_wait(barrier, len(peers) + k)

    sends = []

    def push(src, dst, s, r, device):
        copy = pltpu.make_async_remote_copy(src_ref=src, dst_ref=dst, send_sem=s, recv_sem=r, device_id=device, device_id_type=MESH)
        copy.start()
        sends.append(copy)

    def got(dst, s, r):
        pltpu.make_async_remote_copy(src_ref=dst, dst_ref=dst, send_sem=s, recv_sem=r, device_id=mate, device_id_type=MESH).wait_recv()

    def ag_block(a, zb):
        return ag.at[a, k, pl.ds(block_rows(zb), T), :]

    counts = [0, 0]

    def ag_push(a, zb, d):
        n = counts[a]
        counts[a] = n + 1
        push(ag_block(a, zb), ag_block(a, zb), ag_send.at[a * AG_PER + n], ag_recv.at[a * AG_PER + block_pos(zb)], zdev(d))

    def ag_got(a, zb):
        got(ag_block(a, zb), ag_send.at[0], ag_recv.at[a * AG_PER + block_pos(zb)])

    def half_block(a, zb, h):
        return ag.at[a, k, pl.ds(block_rows(zb), T), h * HALF:(h + 1) * HALF]

    for d in (4, -4, 1, -1):
        ag_push(0, z, d)

    @pl.when(k == 1)
    def _():
        pl.semaphore_signal(mate_sem, inc=1, device_id=mate, device_id_type=MESH)

    cp_mask.wait()
    cp_up.wait()
    for i in range(NB):
        for j in range(NB):
            m = mask_ref[i, j].astype(F32).astype(BF16)
            wup[k, B * i:B * (i + 1), B * j:B * (j + 1)] = wup[k, B * i:B * (i + 1), B * j:B * (j + 1)] * m
    cp_dn.wait()
    for i in range(NB):
        for j in range(NB):
            m = mask_ref[i, j].astype(F32).astype(BF16)
            wdn[k, B * j:B * (j + 1), B * i:B * (i + 1)] = wdn[k, B * j:B * (j + 1), B * i:B * (i + 1)] * m

    def ag_forward(a):
        for h, d in ((0, 4), (1, -4)):
            ag_got(a, z - d)
            n = counts[a]
            counts[a] = n + 1
            push(half_block(a, z - d, h), half_block(a, z - d, h), ag_send.at[a * AG_PER + n], ag_recv.at[a * AG_PER + 16 + h], zdev(d))
            for f in (1, -1):
                ag_push(a, z - d, f)

    def ag_relay(a, dist):
        for f in (1, -1):
            ag_got(a, z - f * dist)
            ag_push(a, z - f * dist, f)

    def ag_opposite(a):
        for h in range(2):
            got(half_block(a, z + 8, h), ag_send.at[0], ag_recv.at[a * AG_PER + 16 + h])
        for f in (1, -1):
            ag_push(a, z + 8, f)

    def ag_rest(a):
        for d in (-3, 3, -7, 7, 2, -2, 6, -6):
            ag_got(a, z + d)
        push(ag.at[a, k], ag.at[a, k], send.at[(D_TOK, D_COT)[a]], recv.at[(D_TOK, D_COT)[a]], mate)

    axes = ((x, xdev, y, ydev), (y, ydev, x, xdev))

    def sem(base, a, h, d):
        i = base + (a * 2 + h) * 3 + d - 1
        return send.at[i], recv.at[i]

    def first_rows(h, d):
        return pl.ds(pl.multiple_of(((axes[h][0] + d) % 4) * 64, 64), 64)

    def second_rows(h, d):
        return pl.ds(pl.multiple_of(axes[h][0] * 64 + ((axes[h][2] + d) % 4) * T, T), T)

    def partial_and_send(a):
        for h in range(2):
            for n in range(N_CH):
                c = slice(n * CH, (n + 1) * CH)
                if a == 0:
                    v = jnp.dot(ag[0, k], wup[h, :, c], preferred_element_type=F32)
                else:
                    v = lax.dot_general(ag[1, k], wdn[h, c, :], (((1,), (1,)), ((), ())), preferred_element_type=F32)
                part[a, h, :, c] = v.astype(BF16)
            for d in (2, 1, 3):
                s, r = sem(S1, a, h, d)
                push(part.at[a, h, first_rows(h, d), :], s1buf.at[a, h, d - 1], s, r, axes[h][1](d))

    def second_stage(a):
        for h in range(2):
            for d in (1, 2, 3):
                got(s1buf.at[a, h, d - 1], *sem(S1, a, h, d))
            total = part[a, h, first_rows(h, 0), :].astype(F32)
            for d in range(3):
                total = total + s1buf[a, h, d].astype(F32)
            part[a, h, first_rows(h, 0), :] = total.astype(BF16)
            for d in (2, 1, 3):
                s, r = sem(S2, a, h, d)
                push(part.at[a, h, second_rows(h, d), :], s2buf.at[a, h, d - 1], s, r, axes[h][3](d))

    def shard(a, h):
        for d in (1, 2, 3):
            got(s2buf.at[a, h, d - 1], *sem(S2, a, h, d))
        total = part[a, h, second_rows(h, 0), :].astype(F32)
        for d in range(3):
            total = total + s2buf[a, h, d].astype(F32)
        return total

    def spread(a, h, value):
        acts[a, h, second_rows(h, 0), :] = value.astype(BF16)
        for d in (2, 1, 3):
            s, r = sem(G1, a, h, d)
            push(acts.at[a, h, second_rows(h, 0), :], acts.at[a, h, second_rows(h, 0), :], s, r, axes[h][3](d))

    def spread_more(a):
        for h in range(2):
            for d in (1, 2, 3):
                got(acts.at[a, h, second_rows(h, -d + 4), :], *sem(G1, a, h, d))
            for d in (2, 1, 3):
                s, r = sem(G2, a, h, d)
                push(acts.at[a, h, first_rows(h, 0), :], acts.at[a, h, first_rows(h, 0), :], s, r, axes[h][1](d))

    def spread_end(a):
        for h in range(2):
            for d in (1, 2, 3):
                got(acts.at[a, h, first_rows(h, -d + 4), :], *sem(G2, a, h, d))

    def z_partial(a):
        for n in range(N_CH):
            c = slice(n * CH, (n + 1) * CH)
            if a == 0:
                v = jnp.dot(acts[0, 0], wdn[0, :, c], preferred_element_type=F32)
                v = v + jnp.dot(acts[0, 1], wdn[1, :, c], preferred_element_type=F32)
            else:
                dims = (((1,), (1,)), ((), ()))
                v = lax.dot_general(acts[1, 0], wup[0, c, :], dims, preferred_element_type=F32)
                v = v + lax.dot_general(acts[1, 1], wup[1, c, :], dims, preferred_element_type=F32)
            zpart[a, :, c] = v.astype(BF16)
        r = R1 + 4 * a
        push(zpart.at[a, pl.ds(pair_rows(z - 2), 32), :], r1buf.at[a, pl.ds(128, 32), :], send.at[r + 2], recv.at[r + 2], zdev(2))
        push(zpart.at[a, pl.ds(pair_rows(z + 2), 32), :], r1buf.at[a, pl.ds(160, 32), :], send.at[r + 3], recv.at[r + 3], zdev(-2))
        push(zpart.at[a, pl.ds(class_rows(z + 1), 64), :], r1buf.at[a, pl.ds(0, 64), :], send.at[r], recv.at[r], zdev(1))
        push(zpart.at[a, pl.ds(class_rows(z - 1), 64), :], r1buf.at[a, pl.ds(64, 64), :], send.at[r + 1], recv.at[r + 1], zdev(-1))
        d = (D_ACT, D_HG)[a]
        push(acts.at[a, other], pacts.at[a], send.at[d], recv.at[d], mate)

    def z_second(a):
        r = R1 + 4 * a
        got(r1buf.at[a, pl.ds(128, 32), :], send.at[r + 2], recv.at[r + 2])
        got(r1buf.at[a, pl.ds(160, 32), :], send.at[r + 3], recv.at[r + 3])
        got(r1buf.at[a, pl.ds(0, 64), :], send.at[r], recv.at[r])
        got(r1buf.at[a, pl.ds(64, 64), :], send.at[r + 1], recv.at[r + 1])
        cls = pl.ds(class_rows(z), 64)
        r1sum[a] = zpart[a, cls, :].astype(F32) + r1buf[a, 0:64, :].astype(F32) + r1buf[a, 64:128, :].astype(F32)
        far = pl.ds(pl.multiple_of(pair_rows(z + 4) - class_rows(z), 32), 32)
        r1sum[a, far, :] = r1sum[a, far, :] + r1buf[a, 128:160, :].astype(F32) + r1buf[a, 160:192, :].astype(F32)
        zpart[a, cls, :] = r1sum[a].astype(BF16)
        q = R2 + 3 * a
        for n, d in enumerate((8, 4, -4)):
            push(zpart.at[a, pl.ds(block_rows(z + d), T), :], r2buf.at[a, n], send.at[q + n], recv.at[q + n], zdev(d))

    def z_end(a):
        q = R2 + 3 * a
        for n in range(3):
            got(r2buf.at[a, n], send.at[q + n], recv.at[q + n])
        total = r1sum[a, pl.ds(pl.multiple_of(block_rows(z) - class_rows(z), T), T), :]
        for n in range(3):
            total = total + r2buf[a, n].astype(F32)
        obuf[a] = total.astype(BF16)

    def grads(a):
        i = (D_ACT, D_HG)[a]
        got(pacts.at[a], send.at[i], recv.at[i])
        dims = (((0,), (0,)), ((), ()))
        for n in range(N_CH):
            c = slice(n * CH, (n + 1) * CH)
            if a == 0:
                v = lax.dot_general(acts[0, k, :, c], ag[1, k], dims, preferred_element_type=F32)
                v = v + lax.dot_general(pacts[0, :, c], ag[1, other], dims, preferred_element_type=F32)
            else:
                v = lax.dot_general(ag[0, k, :, c], acts[1, k], dims, preferred_element_type=F32)
                v = v + lax.dot_general(ag[0, other, :, c], pacts[1], dims, preferred_element_type=F32)
            for i in range(CH // B):
                for j in range(NB):
                    p = n * (CH // B) + i
                    m = (mask_ref[j, p] if a == 0 else mask_ref[p, j]).astype(F32)
                    gbuf[a, B * p:B * (p + 1), B * j:B * (j + 1)] = (v[B * i:B * (i + 1), B * j:B * (j + 1)] * m).astype(BF16)

    ag_forward(0)
    ag_relay(0, 1)
    for d in (4, -4, 1, -1):
        ag_push(1, z, d)

    @pl.when(k == 0)
    def _():
        pl.semaphore_wait(mate_sem, 1)

    push(wup.at[k], wup.at[k], send.at[D_UP], recv.at[D_UP], mate)
    push(wdn.at[k], wdn.at[k], send.at[D_DN], recv.at[D_DN], mate)
    ag_relay(0, 5)
    ag_opposite(0)
    ag_forward(1)
    ag_relay(1, 1)
    ag_rest(0)
    got(wup.at[other], send.at[D_UP], recv.at[D_UP])
    partial_and_send(0)
    ag_relay(1, 5)
    ag_opposite(1)
    second_stage(0)
    ag_rest(1)
    got(wdn.at[other], send.at[D_DN], recv.at[D_DN])
    partial_and_send(1)
    pre = []
    for h in range(2):
        v = shard(0, h)
        t = jnp.tanh(GELU_C * (v + GELU_A * v * v * v))
        spread(0, h, 0.5 * v * (1.0 + t))
        pre.append(0.5 * (1.0 + t) + 0.5 * v * (1.0 - t * t) * (GELU_C * (1.0 + 3.0 * GELU_A * v * v)))
    spread_more(0)
    second_stage(1)
    for h in range(2):
        spread(1, h, pre[h] * shard(1, h))
    spread_end(0)
    z_partial(0)
    spread_more(1)
    got(ag.at[0, other], send.at[D_TOK], recv.at[D_TOK])
    got(ag.at[1, other], send.at[D_COT], recv.at[D_COT])
    z_second(0)
    spread_end(1)
    z_partial(1)
    grads(0)
    cp_dg = pltpu.make_async_copy(gbuf.at[0], dng_hbm, loc.at[0])
    cp_dg.start()
    z_second(1)
    grads(1)
    cp_ug = pltpu.make_async_copy(gbuf.at[1], upg_hbm, loc.at[1])
    cp_ug.start()
    z_end(0)
    cp_out = pltpu.make_async_copy(obuf.at[0], out_hbm, loc.at[2])
    cp_out.start()
    z_end(1)
    cp_in = pltpu.make_async_copy(obuf.at[1], in_hbm, loc.at[3])
    cp_in.start()
    for cp in (cp_dg, cp_ug, cp_out, cp_in):
        cp.wait()
    for copy in sends:
        copy.wait_send()


def move_out(*refs):
    given, taken, held, sems = refs[:4], refs[4:8], refs[8:12], refs[12]
    copies = []
    for g, t, h in zip(given, taken, held):
        rows = min(h.shape[0], 256)
        for r in range(0, h.shape[0], rows):
            copies.append([p.at[pl.ds(r, rows), :] for p in (g, h, t)])
    loads = [pltpu.make_async_copy(g, h, sems.at[0, n]) for n, (g, h, t) in enumerate(copies)]
    stores = [pltpu.make_async_copy(h, t, sems.at[1, n]) for n, (g, h, t) in enumerate(copies)]
    for load in loads:
        load.start()
    for load, store in zip(loads, stores):
        load.wait()
        store.start()
    for store in stores:
        store.wait()


def per_device(tokens, up_proj, down_proj, keep_mask, cotangent):
    hbm = pl.BlockSpec(memory_space=pl.ANY)
    small = jax.ShapeDtypeStruct((T, W), BF16)
    big = jax.ShapeDtypeStruct((W, W), BF16)
    results = pl.pallas_call(
        kernel,
        out_shape=(small, small, big, big),
        in_specs=[pl.BlockSpec(memory_space=pltpu.HBM)] * 5,
        out_specs=(hbm,) * 4,
        scratch_shapes=[
            pltpu.VMEM((2, W, W), BF16),
            pltpu.VMEM((2, W, W), BF16),
            pltpu.VMEM((2, 2, 256, W), BF16),
            pltpu.VMEM((2, 2, 256, W), BF16),
            pltpu.VMEM((2, 2, 3, 64, W), BF16),
            pltpu.VMEM((2, 2, 3, T, W), BF16),
            pltpu.VMEM((2, 2, 256, W), BF16),
            pltpu.VMEM((2, 256, W), BF16),
            pltpu.VMEM((2, 256, W), BF16),
            pltpu.VMEM((2, 192, W), BF16),
            pltpu.VMEM((2, 64, W), F32),
            pltpu.VMEM((2, 3, T, W), BF16),
            pltpu.VMEM((2, W, W), BF16),
            pltpu.VMEM((2, T, W), BF16),
            pltpu.SMEM((NB, NB), jnp.int32),
            pltpu.SemaphoreType.DMA((2 * AG_PER,)),
            pltpu.SemaphoreType.DMA((2 * AG_PER,)),
            pltpu.SemaphoreType.DMA((N_SEM,)),
            pltpu.SemaphoreType.DMA((N_SEM,)),
            pltpu.SemaphoreType.DMA((5,)),
            pltpu.SemaphoreType.REGULAR,
        ],
        compiler_params=pltpu.CompilerParams(collective_id=0, has_side_effects=True, vmem_limit_bytes=60 * 2**20),
        cost_estimate=pl.CostEstimate(flops=3_700_000_000, bytes_accessed=5_000_000, transcendentals=30000),
        name="ffn",
    )(tokens, up_proj, down_proj, keep_mask, cotangent)
    return pl.pallas_call(
        move_out,
        out_shape=(small, small, big, big),
        in_specs=[hbm] * 4,
        out_specs=(hbm,) * 4,
        scratch_shapes=[pltpu.VMEM(r.shape, BF16) for r in (small, small, big, big)] + [pltpu.SemaphoreType.DMA((2, 8))],
        compiler_params=pltpu.CompilerParams(vmem_limit_bytes=60 * 2**20),
        name="move_out",
    )(*results)


def solution(mesh):
    return jax.shard_map(
        per_device,
        mesh=mesh,
        in_specs=(P("col", "row"), P("row", "col"), P("col", "row"), P("row", "col"), P("col", "row")),
        out_specs=(P("col", "row"), P("col", "row"), P("row", "col"), P("col", "row")),
        check_vma=False,
    )
```

```python
import jax
import jax.numpy as jnp
from jax import lax
from jax.experimental import pallas as pl
from jax.experimental.pallas import tpu as pltpu
from jax.sharding import PartitionSpec as P

MESH = pl.DeviceIdType.MESH
F32 = jnp.float32
BF16 = jnp.bfloat16
B = 128
T = 16
W = 768
NB = W // B
HALF = W // 2
CH = 256
N_CH = W // CH

AG_PER = 18
S1, S2, G1, G2 = 0, 12, 24, 36
R1, R2 = 48, 56
D_UP, D_DN, D_TOK, D_COT, D_ACT, D_HG = 62, 63, 64, 65, 66, 67
N_SEM = 68

GELU_C = 0.7978845608028654
GELU_A = 0.044715


def kernel(tok_hbm, up_hbm, down_hbm, mask_hbm, cot_hbm, out_hbm, in_hbm, upg_hbm, dng_hbm,
           wup, wdn, ag, part, s1buf, s2buf, acts, pacts, zpart, r1buf, r1sum, r2buf, gbuf, obuf, mask_ref,
           ag_send, ag_recv, send, recv, loc, mate_sem):
    row = lax.axis_index("row")
    col = lax.axis_index("col")
    x, y = row % 4, row // 4
    z, k = col // 2, col % 2
    other = 1 - k

    def zdev(d):
        return (row, ((z + d + 16) % 16) * 2 + k)

    def xdev(d):
        return (y * 4 + (x + d) % 4, col)

    def ydev(d):
        return (((y + d) % 4) * 4 + x, col)

    mate = (row, z * 2 + other)

    def pair_rows(zb):
        zz = (zb + 32) % 16
        return pl.multiple_of((zz % 4) * 64 + ((zz // 4) % 2) * 32, 32)

    def class_rows(zb):
        return pl.multiple_of(((zb + 32) % 4) * 64, 64)

    def block_pos(zb):
        zz = (zb + 32) % 16
        return (zz % 4) * 4 + ((zz // 4) % 2) * 2 + zz // 8

    def block_rows(zb):
        return pl.multiple_of(block_pos(zb) * T, T)

    mine = pl.ds(block_rows(z), T)
    cp_tok = pltpu.make_async_copy(tok_hbm, ag.at[0, k, mine, :], loc.at[0])
    cp_cot = pltpu.make_async_copy(cot_hbm, ag.at[1, k, mine, :], loc.at[1])
    cp_mask = pltpu.make_async_copy(mask_hbm, mask_ref, loc.at[2])
    cp_up = pltpu.make_async_copy(up_hbm, wup.at[k], loc.at[3])
    cp_dn = pltpu.make_async_copy(down_hbm, wdn.at[k], loc.at[4])
    for cp in (cp_tok, cp_cot, cp_mask, cp_up, cp_dn):
        cp.start()

    peers = [zdev(d) for d in (4, -4, 1, -1, 2, -2)] + [xdev(d) for d in (1, 2, 3)] + [ydev(d) for d in (1, 2, 3)]
    barrier = pltpu.get_barrier_semaphore()
    for peer in peers:
        pl.semaphore_signal(barrier, inc=1, device_id=peer, device_id_type=MESH)

    @pl.when(k == 0)
    def _():
        pl.semaphore_signal(barrier, inc=1, device_id=mate, device_id_type=MESH)

    cp_tok.wait()
    cp_cot.wait()
    pl.semaphore_wait(barrier, len(peers) + k)

    sends = []

    def push(src, dst, s, r, device):
        copy = pltpu.make_async_remote_copy(src_ref=src, dst_ref=dst, send_sem=s, recv_sem=r, device_id=device, device_id_type=MESH)
        copy.start()
        sends.append(copy)

    def got(dst, s, r):
        pltpu.make_async_remote_copy(src_ref=dst, dst_ref=dst, send_sem=s, recv_sem=r, device_id=mate, device_id_type=MESH).wait_recv()

    def ag_block(a, zb):
        return ag.at[a, k, pl.ds(block_rows(zb), T), :]

    counts = [0, 0]

    def ag_push(a, zb, d):
        n = counts[a]
        counts[a] = n + 1
        push(ag_block(a, zb), ag_block(a, zb), ag_send.at[a * AG_PER + n], ag_recv.at[a * AG_PER + block_pos(zb)], zdev(d))

    def ag_got(a, zb):
        got(ag_block(a, zb), ag_send.at[0], ag_recv.at[a * AG_PER + block_pos(zb)])

    def half_block(a, zb, h):
        return ag.at[a, k, pl.ds(block_rows(zb), T), h * HALF:(h + 1) * HALF]

    for d in (4, -4, 1, -1):
        ag_push(0, z, d)

    @pl.when(k == 1)
    def _():
        pl.semaphore_signal(mate_sem, inc=1, device_id=mate, device_id_type=MESH)

    cp_mask.wait()
    cp_up.wait()
    for i in range(NB):
        for j in range(NB):
            m = mask_ref[i, j].astype(F32).astype(BF16)
            wup[k, B * i:B * (i + 1), B * j:B * (j + 1)] = wup[k, B * i:B * (i + 1), B * j:B * (j + 1)] * m
    cp_dn.wait()
    for i in range(NB):
        for j in range(NB):
            m = mask_ref[i, j].astype(F32).astype(BF16)
            wdn[k, B * j:B * (j + 1), B * i:B * (i + 1)] = wdn[k, B * j:B * (j + 1), B * i:B * (i + 1)] * m

    def ag_forward(a):
        for h, d in ((0, 4), (1, -4)):
            ag_got(a, z - d)
            n = counts[a]
            counts[a] = n + 1
            push(half_block(a, z - d, h), half_block(a, z - d, h), ag_send.at[a * AG_PER + n], ag_recv.at[a * AG_PER + 16 + h], zdev(d))
            for f in (1, -1):
                ag_push(a, z - d, f)

    def ag_relay(a, dist):
        for f in (1, -1):
            ag_got(a, z - f * dist)
            ag_push(a, z - f * dist, f)

    def ag_opposite(a):
        for h in range(2):
            got(half_block(a, z + 8, h), ag_send.at[0], ag_recv.at[a * AG_PER + 16 + h])
        for f in (1, -1):
            ag_push(a, z + 8, f)

    def ag_rest(a):
        for d in (-3, 3, -7, 7, 2, -2, 6, -6):
            ag_got(a, z + d)
        push(ag.at[a, k], ag.at[a, k], send.at[(D_TOK, D_COT)[a]], recv.at[(D_TOK, D_COT)[a]], mate)

    axes = ((x, xdev, y, ydev), (y, ydev, x, xdev))

    def sem(base, a, h, d):
        i = base + (a * 2 + h) * 3 + d - 1
        return send.at[i], recv.at[i]

    def first_rows(h, d):
        return pl.ds(pl.multiple_of(((axes[h][0] + d) % 4) * 64, 64), 64)

    def second_rows(h, d):
        return pl.ds(pl.multiple_of(axes[h][0] * 64 + ((axes[h][2] + d) % 4) * T, T), T)

    def partial_and_send(a):
        for h in range(2):
            for n in range(N_CH):
                c = slice(n * CH, (n + 1) * CH)
                if a == 0:
                    v = jnp.dot(ag[0, k], wup[h, :, c], preferred_element_type=F32)
                else:
                    v = lax.dot_general(ag[1, k], wdn[h, c, :], (((1,), (1,)), ((), ())), preferred_element_type=F32)
                part[a, h, :, c] = v.astype(BF16)
            for d in (2, 1, 3):
                s, r = sem(S1, a, h, d)
                push(part.at[a, h, first_rows(h, d), :], s1buf.at[a, h, d - 1], s, r, axes[h][1](d))

    def second_stage(a):
        for h in range(2):
            for d in (1, 2, 3):
                got(s1buf.at[a, h, d - 1], *sem(S1, a, h, d))
            total = part[a, h, first_rows(h, 0), :].astype(F32)
            for d in range(3):
                total = total + s1buf[a, h, d].astype(F32)
            part[a, h, first_rows(h, 0), :] = total.astype(BF16)
            for d in (2, 1, 3):
                s, r = sem(S2, a, h, d)
                push(part.at[a, h, second_rows(h, d), :], s2buf.at[a, h, d - 1], s, r, axes[h][3](d))

    def shard(a, h):
        for d in (1, 2, 3):
            got(s2buf.at[a, h, d - 1], *sem(S2, a, h, d))
        total = part[a, h, second_rows(h, 0), :].astype(F32)
        for d in range(3):
            total = total + s2buf[a, h, d].astype(F32)
        return total

    def spread(a, h, value):
        acts[a, h, second_rows(h, 0), :] = value.astype(BF16)
        for d in (2, 1, 3):
            s, r = sem(G1, a, h, d)
            push(acts.at[a, h, second_rows(h, 0), :], acts.at[a, h, second_rows(h, 0), :], s, r, axes[h][3](d))

    def spread_more(a):
        for h in range(2):
            for d in (1, 2, 3):
                got(acts.at[a, h, second_rows(h, -d + 4), :], *sem(G1, a, h, d))
            for d in (2, 1, 3):
                s, r = sem(G2, a, h, d)
                push(acts.at[a, h, first_rows(h, 0), :], acts.at[a, h, first_rows(h, 0), :], s, r, axes[h][1](d))

    def spread_end(a):
        for h in range(2):
            for d in (1, 2, 3):
                got(acts.at[a, h, first_rows(h, -d + 4), :], *sem(G2, a, h, d))

    def z_partial(a):
        for n in range(N_CH):
            c = slice(n * CH, (n + 1) * CH)
            if a == 0:
                v = jnp.dot(acts[0, 0], wdn[0, :, c], preferred_element_type=F32)
                v = v + jnp.dot(acts[0, 1], wdn[1, :, c], preferred_element_type=F32)
            else:
                dims = (((1,), (1,)), ((), ()))
                v = lax.dot_general(acts[1, 0], wup[0, c, :], dims, preferred_element_type=F32)
                v = v + lax.dot_general(acts[1, 1], wup[1, c, :], dims, preferred_element_type=F32)
            zpart[a, :, c] = v.astype(BF16)
        r = R1 + 4 * a
        push(zpart.at[a, pl.ds(pair_rows(z - 2), 32), :], r1buf.at[a, pl.ds(128, 32), :], send.at[r + 2], recv.at[r + 2], zdev(2))
        push(zpart.at[a, pl.ds(pair_rows(z + 2), 32), :], r1buf.at[a, pl.ds(160, 32), :], send.at[r + 3], recv.at[r + 3], zdev(-2))
        push(zpart.at[a, pl.ds(class_rows(z + 1), 64), :], r1buf.at[a, pl.ds(0, 64), :], send.at[r], recv.at[r], zdev(1))
        push(zpart.at[a, pl.ds(class_rows(z - 1), 64), :], r1buf.at[a, pl.ds(64, 64), :], send.at[r + 1], recv.at[r + 1], zdev(-1))
        d = (D_ACT, D_HG)[a]
        push(acts.at[a, other], pacts.at[a], send.at[d], recv.at[d], mate)

    def z_second(a):
        r = R1 + 4 * a
        got(r1buf.at[a, pl.ds(128, 32), :], send.at[r + 2], recv.at[r + 2])
        got(r1buf.at[a, pl.ds(160, 32), :], send.at[r + 3], recv.at[r + 3])
        got(r1buf.at[a, pl.ds(0, 64), :], send.at[r], recv.at[r])
        got(r1buf.at[a, pl.ds(64, 64), :], send.at[r + 1], recv.at[r + 1])
        cls = pl.ds(class_rows(z), 64)
        r1sum[a] = zpart[a, cls, :].astype(F32) + r1buf[a, 0:64, :].astype(F32) + r1buf[a, 64:128, :].astype(F32)
        far = pl.ds(pl.multiple_of(pair_rows(z + 4) - class_rows(z), 32), 32)
        r1sum[a, far, :] = r1sum[a, far, :] + r1buf[a, 128:160, :].astype(F32) + r1buf[a, 160:192, :].astype(F32)
        zpart[a, cls, :] = r1sum[a].astype(BF16)
        q = R2 + 3 * a
        for n, d in enumerate((8, 4, -4)):
            push(zpart.at[a, pl.ds(block_rows(z + d), T), :], r2buf.at[a, n], send.at[q + n], recv.at[q + n], zdev(d))

    def z_end(a):
        q = R2 + 3 * a
        for n in range(3):
            got(r2buf.at[a, n], send.at[q + n], recv.at[q + n])
        total = r1sum[a, pl.ds(pl.multiple_of(block_rows(z) - class_rows(z), T), T), :]
        for n in range(3):
            total = total + r2buf[a, n].astype(F32)
        obuf[a] = total.astype(BF16)

    def grads(a):
        i = (D_ACT, D_HG)[a]
        got(pacts.at[a], send.at[i], recv.at[i])
        dims = (((0,), (0,)), ((), ()))
        for n in range(N_CH):
            c = slice(n * CH, (n + 1) * CH)
            if a == 0:
                v = lax.dot_general(acts[0, k, :, c], ag[1, k], dims, preferred_element_type=F32)
                v = v + lax.dot_general(pacts[0, :, c], ag[1, other], dims, preferred_element_type=F32)
            else:
                v = lax.dot_general(ag[0, k, :, c], acts[1, k], dims, preferred_element_type=F32)
                v = v + lax.dot_general(ag[0, other, :, c], pacts[1], dims, preferred_element_type=F32)
            for i in range(CH // B):
                for j in range(NB):
                    p = n * (CH // B) + i
                    m = (mask_ref[j, p] if a == 0 else mask_ref[p, j]).astype(F32)
                    gbuf[a, B * p:B * (p + 1), B * j:B * (j + 1)] = (v[B * i:B * (i + 1), B * j:B * (j + 1)] * m).astype(BF16)

    ag_forward(0)
    ag_relay(0, 1)
    for d in (4, -4, 1, -1):
        ag_push(1, z, d)

    @pl.when(k == 0)
    def _():
        pl.semaphore_wait(mate_sem, 1)

    push(wup.at[k], wup.at[k], send.at[D_UP], recv.at[D_UP], mate)
    push(wdn.at[k], wdn.at[k], send.at[D_DN], recv.at[D_DN], mate)
    ag_relay(0, 5)
    ag_opposite(0)
    ag_forward(1)
    ag_relay(1, 1)
    ag_rest(0)
    got(wup.at[other], send.at[D_UP], recv.at[D_UP])
    partial_and_send(0)
    ag_relay(1, 5)
    ag_opposite(1)
    second_stage(0)
    ag_rest(1)
    got(wdn.at[other], send.at[D_DN], recv.at[D_DN])
    partial_and_send(1)
    pre = []
    for h in range(2):
        v = shard(0, h)
        t = jnp.tanh(GELU_C * (v + GELU_A * v * v * v))
        spread(0, h, 0.5 * v * (1.0 + t))
        pre.append(0.5 * (1.0 + t) + 0.5 * v * (1.0 - t * t) * (GELU_C * (1.0 + 3.0 * GELU_A * v * v)))
    second_stage(1)
    spread_more(0)
    for h in range(2):
        spread(1, h, pre[h] * shard(1, h))
    spread_more(1)
    spread_end(0)
    z_partial(0)
    got(ag.at[0, other], send.at[D_TOK], recv.at[D_TOK])
    got(ag.at[1, other], send.at[D_COT], recv.at[D_COT])
    z_second(0)
    spread_end(1)
    z_partial(1)
    grads(0)
    cp_dg = pltpu.make_async_copy(gbuf.at[0], dng_hbm, loc.at[0])
    cp_dg.start()
    z_second(1)
    grads(1)
    cp_ug = pltpu.make_async_copy(gbuf.at[1], upg_hbm, loc.at[1])
    cp_ug.start()
    z_end(0)
    cp_out = pltpu.make_async_copy(obuf.at[0], out_hbm, loc.at[2])
    cp_out.start()
    z_end(1)
    cp_in = pltpu.make_async_copy(obuf.at[1], in_hbm, loc.at[3])
    cp_in.start()
    for cp in (cp_dg, cp_ug, cp_out, cp_in):
        cp.wait()
    for copy in sends:
        copy.wait_send()


def move_out(*refs):
    given, taken, held, sems = refs[:4], refs[4:8], refs[8:12], refs[12]
    copies = []
    for g, t, h in zip(given, taken, held):
        rows = min(h.shape[0], 256)
        for r in range(0, h.shape[0], rows):
            copies.append([p.at[pl.ds(r, rows), :] for p in (g, h, t)])
    loads = [pltpu.make_async_copy(g, h, sems.at[0, n]) for n, (g, h, t) in enumerate(copies)]
    stores = [pltpu.make_async_copy(h, t, sems.at[1, n]) for n, (g, h, t) in enumerate(copies)]
    for load in loads:
        load.start()
    for load, store in zip(loads, stores):
        load.wait()
        store.start()
    for store in stores:
        store.wait()


def per_device(tokens, up_proj, down_proj, keep_mask, cotangent):
    hbm = pl.BlockSpec(memory_space=pl.ANY)
    small = jax.ShapeDtypeStruct((T, W), BF16)
    big = jax.ShapeDtypeStruct((W, W), BF16)
    results = pl.pallas_call(
        kernel,
        out_shape=(small, small, big, big),
        in_specs=[pl.BlockSpec(memory_space=pltpu.HBM)] * 5,
        out_specs=(hbm,) * 4,
        scratch_shapes=[
            pltpu.VMEM((2, W, W), BF16),
            pltpu.VMEM((2, W, W), BF16),
            pltpu.VMEM((2, 2, 256, W), BF16),
            pltpu.VMEM((2, 2, 256, W), BF16),
            pltpu.VMEM((2, 2, 3, 64, W), BF16),
            pltpu.VMEM((2, 2, 3, T, W), BF16),
            pltpu.VMEM((2, 2, 256, W), BF16),
            pltpu.VMEM((2, 256, W), BF16),
            pltpu.VMEM((2, 256, W), BF16),
            pltpu.VMEM((2, 192, W), BF16),
            pltpu.VMEM((2, 64, W), F32),
            pltpu.VMEM((2, 3, T, W), BF16),
            pltpu.VMEM((2, W, W), BF16),
            pltpu.VMEM((2, T, W), BF16),
            pltpu.SMEM((NB, NB), jnp.int32),
            pltpu.SemaphoreType.DMA((2 * AG_PER,)),
            pltpu.SemaphoreType.DMA((2 * AG_PER,)),
            pltpu.SemaphoreType.DMA((N_SEM,)),
            pltpu.SemaphoreType.DMA((N_SEM,)),
            pltpu.SemaphoreType.DMA((5,)),
            pltpu.SemaphoreType.REGULAR,
        ],
        compiler_params=pltpu.CompilerParams(collective_id=0, has_side_effects=True, vmem_limit_bytes=60 * 2**20),
        cost_estimate=pl.CostEstimate(flops=3_700_000_000, bytes_accessed=5_000_000, transcendentals=30000),
        name="ffn",
    )(tokens, up_proj, down_proj, keep_mask, cotangent)
    return pl.pallas_call(
        move_out,
        out_shape=(small, small, big, big),
        in_specs=[hbm] * 4,
        out_specs=(hbm,) * 4,
        scratch_shapes=[pltpu.VMEM(r.shape, BF16) for r in (small, small, big, big)] + [pltpu.SemaphoreType.DMA((2, 8))],
        compiler_params=pltpu.CompilerParams(vmem_limit_bytes=60 * 2**20),
        name="move_out",
    )(*results)


def solution(mesh):
    return jax.shard_map(
        per_device,
        mesh=mesh,
        in_specs=(P("col", "row"), P("row", "col"), P("col", "row"), P("row", "col"), P("col", "row")),
        out_specs=(P("col", "row"), P("col", "row"), P("row", "col"), P("col", "row")),
        check_vma=False,
    )
```

```python
import jax
import jax.numpy as jnp
from jax import lax
from jax.experimental import pallas as pl
from jax.experimental.pallas import tpu as pltpu
from jax.sharding import PartitionSpec as P

MESH = pl.DeviceIdType.MESH
F32 = jnp.float32
BF16 = jnp.bfloat16
B = 128
T = 16
W = 768
NB = W // B
HALF = W // 2
CH = 256
N_CH = W // CH

AG_PER = 18
S1, S2, G1, G2 = 0, 12, 24, 36
R1, R2 = 48, 56
D_UP, D_DN, D_TOK, D_COT, D_ACT, D_HG = 62, 63, 64, 65, 66, 67
N_SEM = 68

GELU_C = 0.7978845608028654
GELU_A = 0.044715


def kernel(tok_hbm, up_hbm, down_hbm, mask_hbm, cot_hbm, out_hbm, in_hbm, upg_hbm, dng_hbm,
           wup, wdn, ag, part, s1buf, s2buf, acts, pacts, zpart, r1buf, r1sum, r2buf, gbuf, obuf, mask_ref,
           ag_send, ag_recv, send, recv, loc, mate_sem):
    row = lax.axis_index("row")
    col = lax.axis_index("col")
    x, y = row % 4, row // 4
    z, k = col // 2, col % 2
    other = 1 - k

    def zdev(d):
        return (row, ((z + d + 16) % 16) * 2 + k)

    def xdev(d):
        return (y * 4 + (x + d) % 4, col)

    def ydev(d):
        return (((y + d) % 4) * 4 + x, col)

    mate = (row, z * 2 + other)

    def pair_rows(zb):
        zz = (zb + 32) % 16
        return pl.multiple_of((zz % 4) * 64 + ((zz // 4) % 2) * 32, 32)

    def class_rows(zb):
        return pl.multiple_of(((zb + 32) % 4) * 64, 64)

    def block_pos(zb):
        zz = (zb + 32) % 16
        return (zz % 4) * 4 + ((zz // 4) % 2) * 2 + zz // 8

    def block_rows(zb):
        return pl.multiple_of(block_pos(zb) * T, T)

    mine = pl.ds(block_rows(z), T)
    cp_tok = pltpu.make_async_copy(tok_hbm, ag.at[0, k, mine, :], loc.at[0])
    cp_cot = pltpu.make_async_copy(cot_hbm, ag.at[1, k, mine, :], loc.at[1])
    cp_mask = pltpu.make_async_copy(mask_hbm, mask_ref, loc.at[2])
    cp_up = pltpu.make_async_copy(up_hbm, wup.at[k], loc.at[3])
    cp_dn = pltpu.make_async_copy(down_hbm, wdn.at[k], loc.at[4])
    for cp in (cp_tok, cp_cot, cp_mask, cp_up, cp_dn):
        cp.start()

    peers = [zdev(d) for d in (4, -4, 1, -1, 2, -2)] + [xdev(d) for d in (1, 2, 3)] + [ydev(d) for d in (1, 2, 3)]
    barrier = pltpu.get_barrier_semaphore()
    for peer in peers:
        pl.semaphore_signal(barrier, inc=1, device_id=peer, device_id_type=MESH)

    @pl.when(k == 0)
    def _():
        pl.semaphore_signal(barrier, inc=1, device_id=mate, device_id_type=MESH)

    cp_tok.wait()
    cp_cot.wait()
    pl.semaphore_wait(barrier, len(peers) + k)

    sends = []

    def push(src, dst, s, r, device):
        copy = pltpu.make_async_remote_copy(src_ref=src, dst_ref=dst, send_sem=s, recv_sem=r, device_id=device, device_id_type=MESH)
        copy.start()
        sends.append(copy)

    def got(dst, s, r):
        pltpu.make_async_remote_copy(src_ref=dst, dst_ref=dst, send_sem=s, recv_sem=r, device_id=mate, device_id_type=MESH).wait_recv()

    def ag_block(a, zb):
        return ag.at[a, k, pl.ds(block_rows(zb), T), :]

    counts = [0, 0]

    def ag_push(a, zb, d):
        n = counts[a]
        counts[a] = n + 1
        push(ag_block(a, zb), ag_block(a, zb), ag_send.at[a * AG_PER + n], ag_recv.at[a * AG_PER + block_pos(zb)], zdev(d))

    def ag_got(a, zb):
        got(ag_block(a, zb), ag_send.at[0], ag_recv.at[a * AG_PER + block_pos(zb)])

    def half_block(a, zb, h):
        return ag.at[a, k, pl.ds(block_rows(zb), T), h * HALF:(h + 1) * HALF]

    for d in (4, -4, 1, -1):
        ag_push(0, z, d)

    @pl.when(k == 1)
    def _():
        pl.semaphore_signal(mate_sem, inc=1, device_id=mate, device_id_type=MESH)

    cp_mask.wait()
    cp_up.wait()
    for i in range(NB):
        for j in range(NB):
            m = mask_ref[i, j].astype(F32).astype(BF16)
            wup[k, B * i:B * (i + 1), B * j:B * (j + 1)] = wup[k, B * i:B * (i + 1), B * j:B * (j + 1)] * m
    cp_dn.wait()
    for i in range(NB):
        for j in range(NB):
            m = mask_ref[i, j].astype(F32).astype(BF16)
            wdn[k, B * j:B * (j + 1), B * i:B * (i + 1)] = wdn[k, B * j:B * (j + 1), B * i:B * (i + 1)] * m

    def ag_forward(a):
        for h, d in ((0, 4), (1, -4)):
            ag_got(a, z - d)
            n = counts[a]
            counts[a] = n + 1
            push(half_block(a, z - d, h), half_block(a, z - d, h), ag_send.at[a * AG_PER + n], ag_recv.at[a * AG_PER + 16 + h], zdev(d))
            for f in (1, -1):
                ag_push(a, z - d, f)

    def ag_relay(a, dist):
        for f in (1, -1):
            ag_got(a, z - f * dist)
            ag_push(a, z - f * dist, f)

    def ag_opposite(a):
        for h in range(2):
            got(half_block(a, z + 8, h), ag_send.at[0], ag_recv.at[a * AG_PER + 16 + h])
        for f in (1, -1):
            ag_push(a, z + 8, f)

    def ag_rest(a):
        for d in (-3, 3, -7, 7, 2, -2, 6, -6):
            ag_got(a, z + d)
        push(ag.at[a, k], ag.at[a, k], send.at[(D_TOK, D_COT)[a]], recv.at[(D_TOK, D_COT)[a]], mate)

    axes = ((x, xdev, y, ydev), (y, ydev, x, xdev))

    def sem(base, a, h, d):
        i = base + (a * 2 + h) * 3 + d - 1
        return send.at[i], recv.at[i]

    def first_rows(h, d):
        return pl.ds(pl.multiple_of(((axes[h][0] + d) % 4) * 64, 64), 64)

    def second_rows(h, d):
        return pl.ds(pl.multiple_of(axes[h][0] * 64 + ((axes[h][2] + d) % 4) * T, T), T)

    def partial_and_send(a):
        for h in range(2):
            for n in range(N_CH):
                c = slice(n * CH, (n + 1) * CH)
                if a == 0:
                    v = jnp.dot(ag[0, k], wup[h, :, c], preferred_element_type=F32)
                else:
                    v = lax.dot_general(ag[1, k], wdn[h, c, :], (((1,), (1,)), ((), ())), preferred_element_type=F32)
                part[a, h, :, c] = v.astype(BF16)
            for d in (2, 1, 3):
                s, r = sem(S1, a, h, d)
                push(part.at[a, h, first_rows(h, d), :], s1buf.at[a, h, d - 1], s, r, axes[h][1](d))

    def second_stage(a):
        for h in range(2):
            for d in (1, 2, 3):
                got(s1buf.at[a, h, d - 1], *sem(S1, a, h, d))
            total = part[a, h, first_rows(h, 0), :].astype(F32)
            for d in range(3):
                total = total + s1buf[a, h, d].astype(F32)
            part[a, h, first_rows(h, 0), :] = total.astype(BF16)
            for d in (2, 1, 3):
                s, r = sem(S2, a, h, d)
                push(part.at[a, h, second_rows(h, d), :], s2buf.at[a, h, d - 1], s, r, axes[h][3](d))

    def shard(a, h):
        for d in (1, 2, 3):
            got(s2buf.at[a, h, d - 1], *sem(S2, a, h, d))
        total = part[a, h, second_rows(h, 0), :].astype(F32)
        for d in range(3):
            total = total + s2buf[a, h, d].astype(F32)
        return total

    def spread(a, h, value):
        acts[a, h, second_rows(h, 0), :] = value.astype(BF16)
        for d in (2, 1, 3):
            s, r = sem(G1, a, h, d)
            push(acts.at[a, h, second_rows(h, 0), :], acts.at[a, h, second_rows(h, 0), :], s, r, axes[h][3](d))

    def spread_more(a):
        for h in range(2):
            for d in (1, 2, 3):
                got(acts.at[a, h, second_rows(h, -d + 4), :], *sem(G1, a, h, d))
            for d in (2, 1, 3):
                s, r = sem(G2, a, h, d)
                push(acts.at[a, h, first_rows(h, 0), :], acts.at[a, h, first_rows(h, 0), :], s, r, axes[h][1](d))

    def spread_end(a):
        for h in range(2):
            for d in (1, 2, 3):
                got(acts.at[a, h, first_rows(h, -d + 4), :], *sem(G2, a, h, d))

    def z_partial(a):
        for n in range(N_CH):
            c = slice(n * CH, (n + 1) * CH)
            if a == 0:
                v = jnp.dot(acts[0, 0], wdn[0, :, c], preferred_element_type=F32)
                v = v + jnp.dot(acts[0, 1], wdn[1, :, c], preferred_element_type=F32)
            else:
                dims = (((1,), (1,)), ((), ()))
                v = lax.dot_general(acts[1, 0], wup[0, c, :], dims, preferred_element_type=F32)
                v = v + lax.dot_general(acts[1, 1], wup[1, c, :], dims, preferred_element_type=F32)
            zpart[a, :, c] = v.astype(BF16)
        r = R1 + 4 * a
        push(zpart.at[a, pl.ds(pair_rows(z - 2), 32), :], r1buf.at[a, pl.ds(128, 32), :], send.at[r + 2], recv.at[r + 2], zdev(2))
        push(zpart.at[a, pl.ds(pair_rows(z + 2), 32), :], r1buf.at[a, pl.ds(160, 32), :], send.at[r + 3], recv.at[r + 3], zdev(-2))
        push(zpart.at[a, pl.ds(class_rows(z + 1), 64), :], r1buf.at[a, pl.ds(0, 64), :], send.at[r], recv.at[r], zdev(1))
        push(zpart.at[a, pl.ds(class_rows(z - 1), 64), :], r1buf.at[a, pl.ds(64, 64), :], send.at[r + 1], recv.at[r + 1], zdev(-1))
        d = (D_ACT, D_HG)[a]
        push(acts.at[a, other], pacts.at[a], send.at[d], recv.at[d], mate)

    def z_second(a):
        r = R1 + 4 * a
        got(r1buf.at[a, pl.ds(128, 32), :], send.at[r + 2], recv.at[r + 2])
        got(r1buf.at[a, pl.ds(160, 32), :], send.at[r + 3], recv.at[r + 3])
        got(r1buf.at[a, pl.ds(0, 64), :], send.at[r], recv.at[r])
        got(r1buf.at[a, pl.ds(64, 64), :], send.at[r + 1], recv.at[r + 1])
        cls = pl.ds(class_rows(z), 64)
        r1sum[a] = zpart[a, cls, :].astype(F32) + r1buf[a, 0:64, :].astype(F32) + r1buf[a, 64:128, :].astype(F32)
        far = pl.ds(pl.multiple_of(pair_rows(z + 4) - class_rows(z), 32), 32)
        r1sum[a, far, :] = r1sum[a, far, :] + r1buf[a, 128:160, :].astype(F32) + r1buf[a, 160:192, :].astype(F32)
        zpart[a, cls, :] = r1sum[a].astype(BF16)
        q = R2 + 3 * a
        for n, d in enumerate((8, 4, -4)):
            push(zpart.at[a, pl.ds(block_rows(z + d), T), :], r2buf.at[a, n], send.at[q + n], recv.at[q + n], zdev(d))

    def z_end(a):
        q = R2 + 3 * a
        for n in range(3):
            got(r2buf.at[a, n], send.at[q + n], recv.at[q + n])
        total = r1sum[a, pl.ds(pl.multiple_of(block_rows(z) - class_rows(z), T), T), :]
        for n in range(3):
            total = total + r2buf[a, n].astype(F32)
        obuf[a] = total.astype(BF16)

    def grads(a):
        i = (D_ACT, D_HG)[a]
        got(pacts.at[a], send.at[i], recv.at[i])
        dims = (((0,), (0,)), ((), ()))
        for n in range(N_CH):
            c = slice(n * CH, (n + 1) * CH)
            if a == 0:
                v = lax.dot_general(acts[0, k, :, c], ag[1, k], dims, preferred_element_type=F32)
                v = v + lax.dot_general(pacts[0, :, c], ag[1, other], dims, preferred_element_type=F32)
            else:
                v = lax.dot_general(ag[0, k, :, c], acts[1, k], dims, preferred_element_type=F32)
                v = v + lax.dot_general(ag[0, other, :, c], pacts[1], dims, preferred_element_type=F32)
            for i in range(CH // B):
                for j in range(NB):
                    p = n * (CH // B) + i
                    m = (mask_ref[j, p] if a == 0 else mask_ref[p, j]).astype(F32)
                    gbuf[a, B * p:B * (p + 1), B * j:B * (j + 1)] = (v[B * i:B * (i + 1), B * j:B * (j + 1)] * m).astype(BF16)

    ag_forward(0)
    ag_relay(0, 1)
    for d in (4, -4, 1, -1):
        ag_push(1, z, d)

    @pl.when(k == 0)
    def _():
        pl.semaphore_wait(mate_sem, 1)

    push(wup.at[k], wup.at[k], send.at[D_UP], recv.at[D_UP], mate)
    push(wdn.at[k], wdn.at[k], send.at[D_DN], recv.at[D_DN], mate)
    ag_relay(0, 5)
    ag_opposite(0)
    ag_forward(1)
    ag_relay(1, 1)
    ag_rest(0)
    got(wup.at[other], send.at[D_UP], recv.at[D_UP])
    partial_and_send(0)
    ag_relay(1, 5)
    ag_opposite(1)
    second_stage(0)
    ag_rest(1)
    got(wdn.at[other], send.at[D_DN], recv.at[D_DN])
    partial_and_send(1)
    pre = []
    for h in range(2):
        v = shard(0, h)
        t = jnp.tanh(GELU_C * (v + GELU_A * v * v * v))
        spread(0, h, 0.5 * v * (1.0 + t))
        pre.append(0.5 * (1.0 + t) + 0.5 * v * (1.0 - t * t) * (GELU_C * (1.0 + 3.0 * GELU_A * v * v)))
    second_stage(1)
    spread_more(0)
    for h in range(2):
        spread(1, h, pre[h] * shard(1, h))
    spread_more(1)
    spread_end(0)
    z_partial(0)
    spread_end(1)
    z_partial(1)
    z_second(0)
    got(ag.at[0, other], send.at[D_TOK], recv.at[D_TOK])
    got(ag.at[1, other], send.at[D_COT], recv.at[D_COT])
    grads(0)
    cp_dg = pltpu.make_async_copy(gbuf.at[0], dng_hbm, loc.at[0])
    cp_dg.start()
    z_second(1)
    grads(1)
    cp_ug = pltpu.make_async_copy(gbuf.at[1], upg_hbm, loc.at[1])
    cp_ug.start()
    z_end(0)
    cp_out = pltpu.make_async_copy(obuf.at[0], out_hbm, loc.at[2])
    cp_out.start()
    z_end(1)
    cp_in = pltpu.make_async_copy(obuf.at[1], in_hbm, loc.at[3])
    cp_in.start()
    for cp in (cp_dg, cp_ug, cp_out, cp_in):
        cp.wait()
    for copy in sends:
        copy.wait_send()


def move_out(*refs):
    given, taken, held, sems = refs[:4], refs[4:8], refs[8:12], refs[12]
    copies = []
    for g, t, h in zip(given, taken, held):
        rows = min(h.shape[0], 256)
        for r in range(0, h.shape[0], rows):
            copies.append([p.at[pl.ds(r, rows), :] for p in (g, h, t)])
    loads = [pltpu.make_async_copy(g, h, sems.at[0, n]) for n, (g, h, t) in enumerate(copies)]
    stores = [pltpu.make_async_copy(h, t, sems.at[1, n]) for n, (g, h, t) in enumerate(copies)]
    for load in loads:
        load.start()
    for load, store in zip(loads, stores):
        load.wait()
        store.start()
    for store in stores:
        store.wait()


def per_device(tokens, up_proj, down_proj, keep_mask, cotangent):
    hbm = pl.BlockSpec(memory_space=pl.ANY)
    small = jax.ShapeDtypeStruct((T, W), BF16)
    big = jax.ShapeDtypeStruct((W, W), BF16)
    results = pl.pallas_call(
        kernel,
        out_shape=(small, small, big, big),
        in_specs=[pl.BlockSpec(memory_space=pltpu.HBM)] * 5,
        out_specs=(hbm,) * 4,
        scratch_shapes=[
            pltpu.VMEM((2, W, W), BF16),
            pltpu.VMEM((2, W, W), BF16),
            pltpu.VMEM((2, 2, 256, W), BF16),
            pltpu.VMEM((2, 2, 256, W), BF16),
            pltpu.VMEM((2, 2, 3, 64, W), BF16),
            pltpu.VMEM((2, 2, 3, T, W), BF16),
            pltpu.VMEM((2, 2, 256, W), BF16),
            pltpu.VMEM((2, 256, W), BF16),
            pltpu.VMEM((2, 256, W), BF16),
            pltpu.VMEM((2, 192, W), BF16),
            pltpu.VMEM((2, 64, W), F32),
            pltpu.VMEM((2, 3, T, W), BF16),
            pltpu.VMEM((2, W, W), BF16),
            pltpu.VMEM((2, T, W), BF16),
            pltpu.SMEM((NB, NB), jnp.int32),
            pltpu.SemaphoreType.DMA((2 * AG_PER,)),
            pltpu.SemaphoreType.DMA((2 * AG_PER,)),
            pltpu.SemaphoreType.DMA((N_SEM,)),
            pltpu.SemaphoreType.DMA((N_SEM,)),
            pltpu.SemaphoreType.DMA((5,)),
            pltpu.SemaphoreType.REGULAR,
        ],
        compiler_params=pltpu.CompilerParams(collective_id=0, has_side_effects=True, vmem_limit_bytes=60 * 2**20),
        cost_estimate=pl.CostEstimate(flops=3_700_000_000, bytes_accessed=5_000_000, transcendentals=30000),
        name="ffn",
    )(tokens, up_proj, down_proj, keep_mask, cotangent)
    return pl.pallas_call(
        move_out,
        out_shape=(small, small, big, big),
        in_specs=[hbm] * 4,
        out_specs=(hbm,) * 4,
        scratch_shapes=[pltpu.VMEM(r.shape, BF16) for r in (small, small, big, big)] + [pltpu.SemaphoreType.DMA((2, 8))],
        compiler_params=pltpu.CompilerParams(vmem_limit_bytes=60 * 2**20),
        name="move_out",
    )(*results)


def solution(mesh):
    return jax.shard_map(
        per_device,
        mesh=mesh,
        in_specs=(P("col", "row"), P("row", "col"), P("col", "row"), P("row", "col"), P("col", "row")),
        out_specs=(P("col", "row"), P("col", "row"), P("row", "col"), P("col", "row")),
        check_vma=False,
    )
```

```python
import jax
import jax.numpy as jnp
from jax import lax
from jax.experimental import pallas as pl
from jax.experimental.pallas import tpu as pltpu
from jax.sharding import PartitionSpec as P

MESH = pl.DeviceIdType.MESH
F32 = jnp.float32
BF16 = jnp.bfloat16
B = 128
T = 16
W = 768
NB = W // B
HALF = W // 2
CH = 256
N_CH = W // CH

AG_PER = 18
S1, S2, G1, G2 = 0, 12, 24, 36
R1, R2 = 48, 56
D_UP, D_DN, D_TOK, D_COT, D_ACT, D_HG = 62, 63, 64, 65, 66, 67
N_SEM = 68

GELU_C = 0.7978845608028654
GELU_A = 0.044715


def kernel(tok_hbm, up_hbm, down_hbm, mask_hbm, cot_hbm, out_hbm, in_hbm, upg_hbm, dng_hbm,
           wup, wdn, ag, part, s1buf, s2buf, acts, pacts, zpart, r1buf, r1sum, r2buf, gbuf, obuf, mask_ref,
           ag_send, ag_recv, send, recv, loc, mate_sem):
    row = lax.axis_index("row")
    col = lax.axis_index("col")
    x, y = row % 4, row // 4
    z, k = col // 2, col % 2
    other = 1 - k

    def zdev(d):
        return (row, ((z + d + 16) % 16) * 2 + k)

    def xdev(d):
        return (y * 4 + (x + d) % 4, col)

    def ydev(d):
        return (((y + d) % 4) * 4 + x, col)

    mate = (row, z * 2 + other)

    def pair_rows(zb):
        zz = (zb + 32) % 16
        return pl.multiple_of((zz % 4) * 64 + ((zz // 4) % 2) * 32, 32)

    def class_rows(zb):
        return pl.multiple_of(((zb + 32) % 4) * 64, 64)

    def block_pos(zb):
        zz = (zb + 32) % 16
        return (zz % 4) * 4 + ((zz // 4) % 2) * 2 + zz // 8

    def block_rows(zb):
        return pl.multiple_of(block_pos(zb) * T, T)

    mine = pl.ds(block_rows(z), T)
    cp_tok = pltpu.make_async_copy(tok_hbm, ag.at[0, k, mine, :], loc.at[0])
    cp_cot = pltpu.make_async_copy(cot_hbm, ag.at[1, k, mine, :], loc.at[1])
    cp_mask = pltpu.make_async_copy(mask_hbm, mask_ref, loc.at[2])
    cp_up = pltpu.make_async_copy(up_hbm, wup.at[k], loc.at[3])
    cp_dn = pltpu.make_async_copy(down_hbm, wdn.at[k], loc.at[4])
    for cp in (cp_tok, cp_cot, cp_mask, cp_up, cp_dn):
        cp.start()

    peers = [zdev(d) for d in (4, -4, 1, -1, 2, -2)] + [xdev(d) for d in (1, 2, 3)] + [ydev(d) for d in (1, 2, 3)]
    barrier = pltpu.get_barrier_semaphore()
    for peer in peers:
        pl.semaphore_signal(barrier, inc=1, device_id=peer, device_id_type=MESH)

    @pl.when(k == 0)
    def _():
        pl.semaphore_signal(barrier, inc=1, device_id=mate, device_id_type=MESH)

    cp_tok.wait()
    cp_cot.wait()
    pl.semaphore_wait(barrier, len(peers) + k)

    sends = []

    def push(src, dst, s, r, device):
        copy = pltpu.make_async_remote_copy(src_ref=src, dst_ref=dst, send_sem=s, recv_sem=r, device_id=device, device_id_type=MESH)
        copy.start()
        sends.append(copy)

    def got(dst, s, r):
        pltpu.make_async_remote_copy(src_ref=dst, dst_ref=dst, send_sem=s, recv_sem=r, device_id=mate, device_id_type=MESH).wait_recv()

    def ag_block(a, zb):
        return ag.at[a, k, pl.ds(block_rows(zb), T), :]

    counts = [0, 0]

    def ag_push(a, zb, d):
        n = counts[a]
        counts[a] = n + 1
        push(ag_block(a, zb), ag_block(a, zb), ag_send.at[a * AG_PER + n], ag_recv.at[a * AG_PER + block_pos(zb)], zdev(d))

    def ag_got(a, zb):
        got(ag_block(a, zb), ag_send.at[0], ag_recv.at[a * AG_PER + block_pos(zb)])

    def half_block(a, zb, h):
        return ag.at[a, k, pl.ds(block_rows(zb), T), h * HALF:(h + 1) * HALF]

    for d in (4, -4, 1, -1):
        ag_push(0, z, d)

    @pl.when(k == 1)
    def _():
        pl.semaphore_signal(mate_sem, inc=1, device_id=mate, device_id_type=MESH)

    cp_mask.wait()
    cp_up.wait()
    for i in range(NB):
        for j in range(NB):
            m = mask_ref[i, j].astype(F32).astype(BF16)
            wup[k, B * i:B * (i + 1), B * j:B * (j + 1)] = wup[k, B * i:B * (i + 1), B * j:B * (j + 1)] * m
    cp_dn.wait()
    for i in range(NB):
        for j in range(NB):
            m = mask_ref[i, j].astype(F32).astype(BF16)
            wdn[k, B * j:B * (j + 1), B * i:B * (i + 1)] = wdn[k, B * j:B * (j + 1), B * i:B * (i + 1)] * m

    def ag_forward(a):
        for h, d in ((0, 4), (1, -4)):
            ag_got(a, z - d)
            n = counts[a]
            counts[a] = n + 1
            push(half_block(a, z - d, h), half_block(a, z - d, h), ag_send.at[a * AG_PER + n], ag_recv.at[a * AG_PER + 16 + h], zdev(d))
            for f in (1, -1):
                ag_push(a, z - d, f)

    def ag_relay(a, dist):
        for f in (1, -1):
            ag_got(a, z - f * dist)
            ag_push(a, z - f * dist, f)

    def ag_opposite(a):
        for h in range(2):
            got(half_block(a, z + 8, h), ag_send.at[0], ag_recv.at[a * AG_PER + 16 + h])
        for f in (1, -1):
            ag_push(a, z + 8, f)

    def ag_rest(a):
        for d in (-3, 3, -7, 7, 2, -2, 6, -6):
            ag_got(a, z + d)
        push(ag.at[a, k], ag.at[a, k], send.at[(D_TOK, D_COT)[a]], recv.at[(D_TOK, D_COT)[a]], mate)

    axes = ((x, xdev, y, ydev), (y, ydev, x, xdev))

    def sem(base, a, h, d):
        i = base + (a * 2 + h) * 3 + d - 1
        return send.at[i], recv.at[i]

    def first_rows(h, d):
        return pl.ds(pl.multiple_of(((axes[h][0] + d) % 4) * 64, 64), 64)

    def second_rows(h, d):
        return pl.ds(pl.multiple_of(axes[h][0] * 64 + ((axes[h][2] + d) % 4) * T, T), T)

    def partial_and_send(a):
        for h in range(2):
            for n in range(N_CH):
                c = slice(n * CH, (n + 1) * CH)
                if a == 0:
                    v = jnp.dot(ag[0, k], wup[h, :, c], preferred_element_type=F32)
                else:
                    v = lax.dot_general(ag[1, k], wdn[h, c, :], (((1,), (1,)), ((), ())), preferred_element_type=F32)
                part[a, h, :, c] = v.astype(BF16)
            for d in (2, 1, 3):
                s, r = sem(S1, a, h, d)
                push(part.at[a, h, first_rows(h, d), :], s1buf.at[a, h, d - 1], s, r, axes[h][1](d))

    def second_stage(a):
        for h in range(2):
            for d in (1, 2, 3):
                got(s1buf.at[a, h, d - 1], *sem(S1, a, h, d))
            total = part[a, h, first_rows(h, 0), :].astype(F32)
            for d in range(3):
                total = total + s1buf[a, h, d].astype(F32)
            part[a, h, first_rows(h, 0), :] = total.astype(BF16)
            for d in (2, 1, 3):
                s, r = sem(S2, a, h, d)
                push(part.at[a, h, second_rows(h, d), :], s2buf.at[a, h, d - 1], s, r, axes[h][3](d))

    def shard(a, h):
        for d in (1, 2, 3):
            got(s2buf.at[a, h, d - 1], *sem(S2, a, h, d))
        total = part[a, h, second_rows(h, 0), :].astype(F32)
        for d in range(3):
            total = total + s2buf[a, h, d].astype(F32)
        return total

    def spread(a, h, value):
        acts[a, h, second_rows(h, 0), :] = value.astype(BF16)
        for d in (2, 1, 3):
            s, r = sem(G1, a, h, d)
            push(acts.at[a, h, second_rows(h, 0), :], acts.at[a, h, second_rows(h, 0), :], s, r, axes[h][3](d))

    def spread_more(a):
        for h in range(2):
            for d in (1, 2, 3):
                got(acts.at[a, h, second_rows(h, -d + 4), :], *sem(G1, a, h, d))
            for d in (2, 1, 3):
                s, r = sem(G2, a, h, d)
                push(acts.at[a, h, first_rows(h, 0), :], acts.at[a, h, first_rows(h, 0), :], s, r, axes[h][1](d))

    def spread_end(a):
        for h in range(2):
            for d in (1, 2, 3):
                got(acts.at[a, h, first_rows(h, -d + 4), :], *sem(G2, a, h, d))

    def z_partial(a):
        for n in range(N_CH):
            c = slice(n * CH, (n + 1) * CH)
            if a == 0:
                v = jnp.dot(acts[0, 0], wdn[0, :, c], preferred_element_type=F32)
                v = v + jnp.dot(acts[0, 1], wdn[1, :, c], preferred_element_type=F32)
            else:
                dims = (((1,), (1,)), ((), ()))
                v = lax.dot_general(acts[1, 0], wup[0, c, :], dims, preferred_element_type=F32)
                v = v + lax.dot_general(acts[1, 1], wup[1, c, :], dims, preferred_element_type=F32)
            zpart[a, :, c] = v.astype(BF16)
        r = R1 + 4 * a
        push(zpart.at[a, pl.ds(pair_rows(z - 2), 32), :], r1buf.at[a, pl.ds(128, 32), :], send.at[r + 2], recv.at[r + 2], zdev(2))
        push(zpart.at[a, pl.ds(pair_rows(z + 2), 32), :], r1buf.at[a, pl.ds(160, 32), :], send.at[r + 3], recv.at[r + 3], zdev(-2))
        push(zpart.at[a, pl.ds(class_rows(z + 1), 64), :], r1buf.at[a, pl.ds(0, 64), :], send.at[r], recv.at[r], zdev(1))
        push(zpart.at[a, pl.ds(class_rows(z - 1), 64), :], r1buf.at[a, pl.ds(64, 64), :], send.at[r + 1], recv.at[r + 1], zdev(-1))
        d = (D_ACT, D_HG)[a]
        push(acts.at[a, other], pacts.at[a], send.at[d], recv.at[d], mate)

    def z_second(a):
        r = R1 + 4 * a
        got(r1buf.at[a, pl.ds(128, 32), :], send.at[r + 2], recv.at[r + 2])
        got(r1buf.at[a, pl.ds(160, 32), :], send.at[r + 3], recv.at[r + 3])
        got(r1buf.at[a, pl.ds(0, 64), :], send.at[r], recv.at[r])
        got(r1buf.at[a, pl.ds(64, 64), :], send.at[r + 1], recv.at[r + 1])
        cls = pl.ds(class_rows(z), 64)
        r1sum[a] = zpart[a, cls, :].astype(F32) + r1buf[a, 0:64, :].astype(F32) + r1buf[a, 64:128, :].astype(F32)
        far = pl.ds(pl.multiple_of(pair_rows(z + 4) - class_rows(z), 32), 32)
        r1sum[a, far, :] = r1sum[a, far, :] + r1buf[a, 128:160, :].astype(F32) + r1buf[a, 160:192, :].astype(F32)
        zpart[a, cls, :] = r1sum[a].astype(BF16)
        q = R2 + 3 * a
        for n, d in enumerate((8, 4, -4)):
            push(zpart.at[a, pl.ds(block_rows(z + d), T), :], r2buf.at[a, n], send.at[q + n], recv.at[q + n], zdev(d))

    def z_end(a):
        q = R2 + 3 * a
        for n in range(3):
            got(r2buf.at[a, n], send.at[q + n], recv.at[q + n])
        total = r1sum[a, pl.ds(pl.multiple_of(block_rows(z) - class_rows(z), T), T), :]
        for n in range(3):
            total = total + r2buf[a, n].astype(F32)
        obuf[a] = total.astype(BF16)

    def grads(a):
        i = (D_ACT, D_HG)[a]
        got(pacts.at[a], send.at[i], recv.at[i])
        dims = (((0,), (0,)), ((), ()))
        for n in range(N_CH):
            c = slice(n * CH, (n + 1) * CH)
            if a == 0:
                v = lax.dot_general(acts[0, k, :, c], ag[1, k], dims, preferred_element_type=F32)
                v = v + lax.dot_general(pacts[0, :, c], ag[1, other], dims, preferred_element_type=F32)
            else:
                v = lax.dot_general(ag[0, k, :, c], acts[1, k], dims, preferred_element_type=F32)
                v = v + lax.dot_general(ag[0, other, :, c], pacts[1], dims, preferred_element_type=F32)
            for i in range(CH // B):
                for j in range(NB):
                    p = n * (CH // B) + i
                    m = (mask_ref[j, p] if a == 0 else mask_ref[p, j]).astype(F32)
                    gbuf[a, B * p:B * (p + 1), B * j:B * (j + 1)] = (v[B * i:B * (i + 1), B * j:B * (j + 1)] * m).astype(BF16)

    ag_forward(0)
    ag_relay(0, 1)
    for d in (4, -4, 1, -1):
        ag_push(1, z, d)

    @pl.when(k == 0)
    def _():
        pl.semaphore_wait(mate_sem, 1)

    push(wup.at[k], wup.at[k], send.at[D_UP], recv.at[D_UP], mate)
    push(wdn.at[k], wdn.at[k], send.at[D_DN], recv.at[D_DN], mate)
    ag_relay(0, 5)
    ag_opposite(0)
    ag_forward(1)
    ag_relay(1, 1)
    ag_rest(0)
    got(wup.at[other], send.at[D_UP], recv.at[D_UP])
    partial_and_send(0)
    ag_relay(1, 5)
    ag_opposite(1)
    second_stage(0)
    ag_rest(1)
    got(wdn.at[other], send.at[D_DN], recv.at[D_DN])
    partial_and_send(1)
    pre = []
    for h in range(2):
        v = shard(0, h)
        t = jnp.tanh(GELU_C * (v + GELU_A * v * v * v))
        spread(0, h, 0.5 * v * (1.0 + t))
        pre.append(0.5 * (1.0 + t) + 0.5 * v * (1.0 - t * t) * (GELU_C * (1.0 + 3.0 * GELU_A * v * v)))
    second_stage(1)
    spread_more(0)
    for h in range(2):
        spread(1, h, pre[h] * shard(1, h))
    spread_more(1)
    spread_end(0)
    z_partial(0)
    spread_end(1)
    z_partial(1)
    z_second(0)
    z_second(1)
    got(ag.at[0, other], send.at[D_TOK], recv.at[D_TOK])
    got(ag.at[1, other], send.at[D_COT], recv.at[D_COT])
    grads(0)
    cp_dg = pltpu.make_async_copy(gbuf.at[0], dng_hbm, loc.at[0])
    cp_dg.start()
    grads(1)
    cp_ug = pltpu.make_async_copy(gbuf.at[1], upg_hbm, loc.at[1])
    cp_ug.start()
    z_end(0)
    cp_out = pltpu.make_async_copy(obuf.at[0], out_hbm, loc.at[2])
    cp_out.start()
    z_end(1)
    cp_in = pltpu.make_async_copy(obuf.at[1], in_hbm, loc.at[3])
    cp_in.start()
    for cp in (cp_dg, cp_ug, cp_out, cp_in):
        cp.wait()
    for copy in sends:
        copy.wait_send()


def move_out(*refs):
    given, taken, held, sems = refs[:4], refs[4:8], refs[8:12], refs[12]
    copies = []
    for g, t, h in zip(given, taken, held):
        rows = min(h.shape[0], 256)
        for r in range(0, h.shape[0], rows):
            copies.append([p.at[pl.ds(r, rows), :] for p in (g, h, t)])
    loads = [pltpu.make_async_copy(g, h, sems.at[0, n]) for n, (g, h, t) in enumerate(copies)]
    stores = [pltpu.make_async_copy(h, t, sems.at[1, n]) for n, (g, h, t) in enumerate(copies)]
    for load in loads:
        load.start()
    for load, store in zip(loads, stores):
        load.wait()
        store.start()
    for store in stores:
        store.wait()


def per_device(tokens, up_proj, down_proj, keep_mask, cotangent):
    hbm = pl.BlockSpec(memory_space=pl.ANY)
    small = jax.ShapeDtypeStruct((T, W), BF16)
    big = jax.ShapeDtypeStruct((W, W), BF16)
    results = pl.pallas_call(
        kernel,
        out_shape=(small, small, big, big),
        in_specs=[pl.BlockSpec(memory_space=pltpu.HBM)] * 5,
        out_specs=(hbm,) * 4,
        scratch_shapes=[
            pltpu.VMEM((2, W, W), BF16),
            pltpu.VMEM((2, W, W), BF16),
            pltpu.VMEM((2, 2, 256, W), BF16),
            pltpu.VMEM((2, 2, 256, W), BF16),
            pltpu.VMEM((2, 2, 3, 64, W), BF16),
            pltpu.VMEM((2, 2, 3, T, W), BF16),
            pltpu.VMEM((2, 2, 256, W), BF16),
            pltpu.VMEM((2, 256, W), BF16),
            pltpu.VMEM((2, 256, W), BF16),
            pltpu.VMEM((2, 192, W), BF16),
            pltpu.VMEM((2, 64, W), F32),
            pltpu.VMEM((2, 3, T, W), BF16),
            pltpu.VMEM((2, W, W), BF16),
            pltpu.VMEM((2, T, W), BF16),
            pltpu.SMEM((NB, NB), jnp.int32),
            pltpu.SemaphoreType.DMA((2 * AG_PER,)),
            pltpu.SemaphoreType.DMA((2 * AG_PER,)),
            pltpu.SemaphoreType.DMA((N_SEM,)),
            pltpu.SemaphoreType.DMA((N_SEM,)),
            pltpu.SemaphoreType.DMA((5,)),
            pltpu.SemaphoreType.REGULAR,
        ],
        compiler_params=pltpu.CompilerParams(collective_id=0, has_side_effects=True, vmem_limit_bytes=60 * 2**20),
        cost_estimate=pl.CostEstimate(flops=3_700_000_000, bytes_accessed=5_000_000, transcendentals=30000),
        name="ffn",
    )(tokens, up_proj, down_proj, keep_mask, cotangent)
    return pl.pallas_call(
        move_out,
        out_shape=(small, small, big, big),
        in_specs=[hbm] * 4,
        out_specs=(hbm,) * 4,
        scratch_shapes=[pltpu.VMEM(r.shape, BF16) for r in (small, small, big, big)] + [pltpu.SemaphoreType.DMA((2, 8))],
        compiler_params=pltpu.CompilerParams(vmem_limit_bytes=60 * 2**20),
        name="move_out",
    )(*results)


def solution(mesh):
    return jax.shard_map(
        per_device,
        mesh=mesh,
        in_specs=(P("col", "row"), P("row", "col"), P("col", "row"), P("row", "col"), P("col", "row")),
        out_specs=(P("col", "row"), P("col", "row"), P("row", "col"), P("col", "row")),
        check_vma=False,
    )
```
